256 devices in a mesh: ens: 8 (over z_lo, x), lat: 32 (over y, z_hi, core).
Axes of the slice: x: 4, y: 4, z: 8 (z_hi: 4, z_lo: 2; z = z_hi * 2 + z_lo), core: 2. Of those that a mesh axis runs over, the one named last changes fastest.
Arguments:
- members: float32 [160, 8, 64, 640], P('lat', 'ens'), may hold values from -24 to 24
- truth: float32 [4, 160, 64, 640], P(None, 'lat'), may hold values from -32 to 32
- target_time: int32 [160], P('lat'), may hold values from 0 to 3
- row_taps: int32 [1, 160, 5], P(None, 'lat'), may hold values from 0 to 159, as said below
- filters: float32 [1, 160, 5, 9, 5], P(None, 'lat'), may hold values from -1.2 to 1.2
- mixing: float32 [1, 64, 9, 64], replicated, may hold values from -0.25 to 0.25
Outputs:
- score_grad: float32 [160, 8, 64, 640], P('lat', 'ens')
- loss_value: float32 [1], replicated
The draws below stay inside these ranges and needn't reach their ends.
Inputs may be any that keep to these rules, and one draw needn't show every extreme that they name: row_taps[l, i, t] lies within 4 rows of i; in every layer some row lists a row exactly 4 below it and some row one exactly 4 above it. `target_time`: selects one of the stored target fields for each latitude row.
All inputs are finite; a program needn't handle non-finite values.
Results may differ from the reference program's by a relative error of at most 0.0003.
Values sent between devices are 32-bit elements; how exact they have to be, the bound alone decides.
A program may use at most 64 MiB of HBM per device.

```python
import math
import jax
import jax.numpy as jnp
from jax import lax

C = 64
NLON = 640
K = 9
TAPS = 5
LW = 5
REACH = 4
LAYERS = 1
TIMES = 4
ENS = 8
NLAT = 160


def draw_row_taps(key, part):
    key_offsets = jax.random.fold_in(key, 11)
    key_chosen = jax.random.fold_in(key, 12)
    row_ids = jnp.arange(NLAT, dtype=jnp.int32)[None, :, None]
    tap_slots = jnp.arange(TAPS, dtype=jnp.int32)[None, None, :]
    offsets = jax.random.randint(key_offsets, (LAYERS, NLAT, TAPS), -REACH, REACH + 1, dtype=jnp.int32)
    chosen = jax.random.randint(key_chosen, (LAYERS, 2), REACH, NLAT - REACH, dtype=jnp.int32)
    upper_mask = (row_ids == chosen[:, 0][:, None, None]) & (tap_slots == 0)
    lower_mask = (row_ids == chosen[:, 1][:, None, None]) & (tap_slots == 1)
    offsets = jnp.where(upper_mask, -REACH, offsets)
    offsets = jnp.where(lower_mask, REACH, offsets)
    return jnp.clip(row_ids + offsets, 0, NLAT - 1).astype(jnp.int32)


def draw_members(key, part):
    key_noise = jax.random.fold_in(key, 21)
    fraction = jnp.arange(ENS, dtype=jnp.float32) / (ENS - 1.0)
    scales = 6.0 ** fraction
    noise = jnp.clip(jax.random.normal(key_noise, (NLAT, ENS, C, NLON), jnp.float32), -4.0, 4.0)
    return (noise * scales[None, :, None, None]).astype(jnp.float32)


def draw_truth(key, part):
    key_noise = jax.random.fold_in(key, 31)
    fraction = jnp.arange(NLON, dtype=jnp.float32) / (NLON - 1.0)
    scales = 8.0 ** fraction
    noise = jnp.clip(jax.random.normal(key_noise, (TIMES, NLAT, C, NLON), jnp.float32), -4.0, 4.0)
    return (noise * scales[None, None, None, :]).astype(jnp.float32)


def touch_ends(array, own_key, low, largest):
    longest = array.shape.index(max(array.shape))
    spots = []
    for shift in (0, 1):
        where = [jax.random.randint(jax.random.fold_in(own_key, axis), (), 0, length) for axis, length in enumerate(array.shape)]
        where[longest] = (where[longest] + shift) % array.shape[longest]
        spots.append(tuple(where))
    return array.at[spots[0]].set(low).at[spots[1]].set(largest)


def level_of(rng, shape, split, smallest, largest):
    def one(axis_at, blocks):
        draws = jax.random.uniform(jax.random.fold_in(jax.random.fold_in(rng, 6), axis_at), (blocks,), jnp.float32, smallest / len(split), largest / len(split))
        return jnp.repeat(jnp.exp(draws), shape[axis_at] // blocks).reshape((-1,) + (1,) * (len(shape) - axis_at - 1))

    gain = one(*split[0])
    for cut in split[1:]:
        gain = gain * one(*cut)
    return gain


def bell_draw(own_key, extent, scale, limit, shards=(), kind=jnp.bfloat16):
    factor_of = level_of(own_key, extent, shards, -0.22, 0.18) if shards else 1.0
    array = jax.random.normal(own_key, extent, jnp.float32) * scale * factor_of
    return jnp.minimum(jnp.maximum(array, -limit), limit).astype(kind)


def setup_inputs(seed: int = 0) -> dict:
    key_list = jax.random.split(jax.random.key(seed), 7)
    members = draw_members(jax.random.fold_in(key_list[6], 71), 0)
    truth = draw_truth(jax.random.fold_in(key_list[6], 71), 0)
    target_time = touch_ends(jax.random.randint(key_list[2], (NLAT,), 0, TIMES), jax.random.fold_in(key_list[2], 1), 0, TIMES - 1).astype(jnp.int32)
    row_taps = draw_row_taps(jax.random.fold_in(key_list[6], 71), 0)
    filters = bell_draw(key_list[4], (LAYERS, NLAT, TAPS, K, LW), 0.2, 1.2, ((1, 32),), jnp.float32)
    mixing = bell_draw(key_list[5], (LAYERS, C, K, C), (K * C) ** -0.5, 0.25, (), jnp.float32)
    return {"members": members, "truth": truth, "target_time": target_time, "row_taps": row_taps, "filters": filters, "mixing": mixing}


def reference(members, truth, target_time, row_taps, filters, mixing):
    highest = lax.Precision.HIGHEST
    half_width = LW // 2
    fields = members
    for layer_number in range(LAYERS):
        weight = mixing[layer_number]

        def one_row(row_inputs):
            tap_rows, row_filter = row_inputs
            picked = jnp.take(fields, tap_rows.astype(jnp.int32), axis=0)
            shifted = jnp.stack([jnp.roll(picked, half_width - lon_lag, axis=-1) for lon_lag in range(LW)], axis=1)
            basis_out = jnp.einsum('tkd,tdmcj->kmcj', row_filter.astype(jnp.float32), shifted.astype(jnp.float32), precision=highest)
            return jnp.einsum('okc,kmcj->moj', weight.astype(jnp.float32), basis_out, precision=highest)
        mixed_out = lax.map(one_row, (row_taps[layer_number], filters[layer_number]))
        fields = fields + jax.nn.gelu(mixed_out, approximate=True)
    row_index = jnp.arange(NLAT, dtype=jnp.int32)
    target = truth[target_time.astype(jnp.int32), row_index]
    latitude = (jnp.arange(NLAT, dtype=jnp.float32) + 0.5) * (math.pi / NLAT) - 0.5 * math.pi
    cosine = jnp.cos(latitude)
    area = cosine / jnp.mean(cosine)
    to_truth = fields - target[:, None]
    skill_dist = jnp.sqrt(lax.optimization_barrier(jnp.mean(to_truth * to_truth, axis=2)) + 1.0)

    def pair_terms(member):
        gap_field = member[:, None] - fields
        distance = jnp.sqrt(lax.optimization_barrier(jnp.mean(gap_field * gap_field, axis=2)) + 1.0)
        return (lax.optimization_barrier(jnp.sum(gap_field / distance[:, :, None], axis=1)), lax.optimization_barrier(jnp.sum(distance, axis=1)))
    pull_sum, spread = lax.map(pair_terms, jnp.moveaxis(fields, 1, 0))
    score_grad = area[:, None, None, None] * (to_truth / skill_dist[:, :, None] - jnp.moveaxis(pull_sum, 0, 1) / ENS)
    per_cell = lax.optimization_barrier(jnp.sum(skill_dist, axis=1)) / ENS - lax.optimization_barrier(jnp.sum(spread, axis=0)) / (2.0 * ENS * ENS)
    loss_value = jnp.sum(area[:, None] * per_cell) / (NLAT * NLON)
    return (score_grad, jnp.reshape(loss_value, (1,)))
```

```python
import functools
import math

import jax
import jax.numpy as jnp
from jax import lax
from jax.experimental import pallas as pl
from jax.experimental.pallas import tpu as pltpu
from jax.sharding import PartitionSpec as P

C = 64
NLON = 640
K = 9
KP = 16
TAPS = 5
LW = 5
REACH = 4
ROWS = 5
LANE = 128
NB = NLON // LANE
BLOCKS = ROWS * NB
SIDE = REACH * C
OWN = ROWS * C
OWN_PAD = 384
BAND = LW * C
MESH = pl.DeviceIdType.MESH
CHUNKS = ((0, 256), (256, 256), (512, 128))
F32 = jnp.float32
BF16 = jnp.bfloat16


def split(x):
    hi = x.astype(BF16)
    return hi, (x - hi.astype(F32)).astype(BF16)


def dot3(w_hi, w_lo, x_hi, x_lo):
    dot = functools.partial(jnp.dot, preferred_element_type=F32)
    return dot(w_hi, x_hi) + dot(w_hi, x_lo) + dot(w_lo, x_hi)


def block_place(b):
    return lax.rem(b, ROWS), lax.rem(b // ROWS + 1, NB)


def kernel(
    n_ens,
    n_lat,
    taps_ref,
    time_ref,
    area_ref,
    filt_ref,
    mix_ref,
    members_ref,
    truth_ref,
    out_ref,
    loss_ref,
    own,
    halo,
    own_hi,
    own_lo,
    side_hi,
    side_lo,
    mdup,
    a_own,
    a_side,
    w_own_hi,
    w_own_lo,
    w_side_hi,
    w_side_lo,
    acc,
    states,
    recv,
    grads,
    cand,
    target,
    lossbuf1,
    lossbuf2,
    lossbuf3,
    own_sem,
    cand_sem,
    halo_send,
    halo_recv,
    fwd_send,
    fwd_recv,
    back_send,
    back_recv,
    self_sem,
    l1_send,
    l1_recv,
    l2_send,
    l2_recv,
    l3_send,
    l3_recv,
):
    me = lax.axis_index("ens")
    lat = lax.axis_index("lat")
    group = min(8, n_lat)
    tall = n_lat // group
    first = lat * ROWS
    core = lax.rem(lat, 2)
    near = 1 - core
    far = core
    slots = BLOCKS // n_ens
    extra = lax.rem(core * (n_ens // 2) + lax.rem(lat // 2, n_ens // 2), n_ens)
    inner = lax.rem(lat, group)
    outer = lat // group
    has_up = lat < n_lat - 1
    has_down = lat > 0

    def place(ens_at, lat_at):
        return {"ens": ens_at, "lat": lat_at}

    def ens_peer(k):
        return lax.rem(me + k, n_ens)

    def inner_peer(k):
        return outer * group + lax.rem(inner + k, group)

    def outer_peer(k):
        return lax.rem(outer + k, tall) * group + inner

    own_copy = pltpu.make_async_copy(members_ref.at[:, 0], own, own_sem)
    own_copy.start()

    def cand_copy(s):
        r, lon = block_place(n_ens * s + me)
        return pltpu.make_async_copy(
            truth_ref.at[:, r, :, pl.ds(pl.multiple_of(lon * LANE, LANE), LANE)], cand.at[s], cand_sem.at[s]
        )

    for s in range(slots):
        cand_copy(s).start()

    @pl.when(me == extra)
    def _():
        r, lon = ROWS - 1, 0
        pltpu.make_async_copy(truth_ref.at[:, r, :, pl.ds(lon, LANE)], cand.at[slots], cand_sem.at[slots]).start()

    barrier = pltpu.get_barrier_semaphore()
    for k in range(1, n_ens):
        pl.semaphore_signal(barrier, inc=1, device_id=place(ens_peer(k), lat), device_id_type=MESH)
    for k in range(1, group):
        pl.semaphore_signal(barrier, inc=1, device_id=place(me, inner_peer(k)), device_id_type=MESH)
    for k in range(1, tall):
        pl.semaphore_signal(barrier, inc=1, device_id=place(me, outer_peer(k)), device_id_type=MESH)
    over_up = has_up & (inner == group - 1)
    over_down = has_down & (inner == 0)

    @pl.when(over_up)
    def _():
        pl.semaphore_signal(barrier, inc=1, device_id=place(me, lat + 1), device_id_type=MESH)

    @pl.when(over_down)
    def _():
        pl.semaphore_signal(barrier, inc=1, device_id=place(me, lat - 1), device_id_type=MESH)

    greeted = n_ens - 1 + group - 1 + tall - 1
    pl.semaphore_wait(barrier, greeted + over_up.astype(jnp.int32) + over_down.astype(jnp.int32))

    def halo_copy(side, chunk):
        start, width = CHUNKS[chunk]
        rows = pl.ds(1, REACH) if side == 0 else pl.ds(0, REACH)
        to = lat + 1 if side == 0 else lat - 1
        return pltpu.make_async_remote_copy(
            src_ref=members_ref.at[rows, 0, :, pl.ds(start, width)],
            dst_ref=halo.at[side, :, :, pl.ds(start, width)],
            send_sem=halo_send.at[side, chunk],
            recv_sem=halo_recv.at[side, chunk],
            device_id=place(me, to),
            device_id_type=MESH,
        )

    def send_side(side):
        for chunk in range(len(CHUNKS)):
            halo_copy(side, chunk).start()

    @pl.when((core == 1) & has_up)
    def _():
        send_side(0)

    @pl.when((core == 0) & has_down)
    def _():
        send_side(1)

    @pl.when((core == 0) & has_up)
    def _():
        send_side(0)

    @pl.when((core == 1) & has_down)
    def _():
        send_side(1)

    @pl.when(jnp.logical_not(has_down))
    def _():
        halo[0] = jnp.zeros_like(halo[0])

    @pl.when(jnp.logical_not(has_up))
    def _():
        halo[1] = jnp.zeros_like(halo[1])

    for k in range(K):
        mdup[k] = jnp.concatenate([mix_ref[k], mix_ref[k]], axis=1)

    def row_of(width, low, high):
        lane = lax.broadcasted_iota(jnp.int32, (1, width), 1)
        q = low + lane // C
        return jnp.where(q < high, q, -1)

    q_own = row_of(OWN_PAD, REACH, REACH + ROWS)
    q_sides = (row_of(SIDE, 0, REACH), row_of(SIDE, REACH + ROWS, ROWS + 2 * REACH))

    def spread(r, q):
        total = None
        for t in range(TAPS):
            hit = (q == taps_ref[r * TAPS + t] - first + REACH).astype(F32)
            term = filt_ref[r, :, t : t + 1] * hit
            total = term if total is None else total + term
        return total

    @pl.loop(0, ROWS)
    def _(r):
        wide = spread(r, q_own)
        low = spread(r, q_sides[0])
        high = spread(r, q_sides[1])
        for d in range(LW):
            a_own[r * LW + d] = wide[d * KP : (d + 1) * KP]
            a_side[0, r * LW + d] = low[d * KP : (d + 1) * KP]
            a_side[1, r * LW + d] = high[d * KP : (d + 1) * KP]

    def weights(rd, a_at, width):
        for at in range(0, width, LANE):
            total = None
            for k in range(K):
                term = a_at[rd, k : k + 1, at : at + LANE] * mdup[k]
                total = term if total is None else total + term
            yield at, split(total)

    @pl.loop(0, ROWS * LW)
    def _(rd):
        rows = pl.ds(pl.multiple_of(rd * C, C), C)
        for at, (hi, lo) in weights(rd, a_own, OWN_PAD):
            w_own_hi[rows, at : at + LANE] = hi
            w_own_lo[rows, at : at + LANE] = lo

    own_copy.wait()
    hi, lo = split(own[...].reshape(OWN, NLON))
    own_hi[:OWN] = hi
    own_lo[:OWN] = lo
    own_hi[OWN:] = jnp.zeros((OWN_PAD - OWN, NLON), BF16)
    own_lo[OWN:] = jnp.zeros((OWN_PAD - OWN, NLON), BF16)

    @pl.loop(0, ROWS)
    def _(r):
        rows = pl.ds(pl.multiple_of(r * BAND, BAND), BAND)
        for start, width in CHUNKS:
            lons = pl.ds(start, width)
            acc[rows, lons] = dot3(w_own_hi[rows, :], w_own_lo[rows, :], own_hi[:, lons], own_lo[:, lons])

    def side_weights(side):
        a_at = a_side.at[side]

        @pl.loop(0, REACH * LW)
        def _(i):
            rows = pl.ds(pl.multiple_of(i * C, C), C)
            for at, (hi, lo) in weights(i + side * LW, a_at, SIDE):
                w_side_hi[rows, at : at + LANE] = hi
                w_side_lo[rows, at : at + LANE] = lo

    def wait_halo(side, chunk):
        @pl.when((side == 0) & has_down)
        def _():
            halo_copy(0, chunk).wait_recv()

        @pl.when((side == 1) & has_up)
        def _():
            halo_copy(1, chunk).wait_recv()

    def add_side(side, chunk):
        start, width = CHUNKS[chunk]
        lons = pl.ds(start, width)
        hi, lo = split(halo[side, :, :, lons].reshape(SIDE, width))
        side_hi[:, lons] = hi
        side_lo[:, lons] = lo

        @pl.loop(0, REACH)
        def _(i):
            rows = pl.ds(pl.multiple_of(i * BAND, BAND), BAND)
            acc_rows = pl.ds(pl.multiple_of((i + side) * BAND, BAND), BAND)
            acc[acc_rows, lons] += dot3(w_side_hi[rows, :], w_side_lo[rows, :], side_hi[:, lons], side_lo[:, lons])

    side_weights(near)
    for chunk in range(len(CHUNKS)):
        wait_halo(near, chunk)
        add_side(near, chunk)
    side_weights(far)

    def pick_target(s, r):
        time = time_ref[r]
        picked = cand[s, 0]
        for t in range(1, 4):
            picked = jnp.where(time == t, cand[s, t], picked)
        target[s] = picked

    for s in range(slots):
        cand_copy(s).wait()
        pick_target(s, lax.rem(n_ens * s + me, ROWS))

    @pl.when(me == extra)
    def _():
        pltpu.make_async_copy(truth_ref.at[:, ROWS - 1, :, pl.ds(0, LANE)], cand.at[slots], cand_sem.at[slots]).wait()
        pick_target(slots, ROWS - 1)

    lane = lax.broadcasted_iota(jnp.int32, (C, LANE), 1)

    def finish(lon, first_block):
        @pl.loop(0, ROWS)
        def _(r):
            def part(d, at):
                rows = pl.ds(pl.multiple_of(r * BAND + d * C, C), C)
                return acc[rows, at * LANE : (at + 1) * LANE]

            total = part(2, lon)
            for d in (0, 1, 3, 4):
                shift = d - LW // 2
                if shift > 0:
                    mine = jnp.where(lane < shift, part(d, (lon + 1) % NB), part(d, lon))
                else:
                    mine = jnp.where(lane >= LANE + shift, part(d, (lon - 1) % NB), part(d, lon))
                total = total + pltpu.roll(mine, (-shift) % LANE, 1)
            cube = total + 0.044715 * total * total * total
            gelu = 0.5 * total * (1.0 + jnp.tanh(math.sqrt(2.0 / math.pi) * cube))
            states[first_block + r] = own[r, :, lon * LANE : (lon + 1) * LANE] + gelu

    def fwd_copy(s, to, source):
        return pltpu.make_async_remote_copy(
            src_ref=states.at[n_ens * s + to] if s < slots else states.at[BLOCKS - 1],
            dst_ref=recv.at[s, source],
            send_sem=fwd_send.at[s, to],
            recv_sem=fwd_recv.at[s, source],
            device_id=place(to, lat),
            device_id_type=MESH,
        )

    def send_slot(s):
        for k in range(1, n_ens):
            fwd_copy(s, ens_peer(k), me).start()
        recv[s, me] = states[n_ens * s + me]

    for chunk in (0, 1):
        wait_halo(far, chunk)
        add_side(far, chunk)
    finish(1, 0)
    finish(2, 5)
    send_slot(0)
    wait_halo(far, 2)
    add_side(far, 2)
    finish(3, 10)
    for s in range(1, slots):
        if n_ens * (s + 1) <= 15:
            send_slot(s)
    finish(4, 15)
    finish(0, 20)
    for s in range(1, slots):
        if n_ens * (s + 1) > 15:
            send_slot(s)

    @pl.when(me != extra)
    def _():
        fwd_copy(slots, extra, me).start()

    pairs = [(a, b) for a in range(n_ens) for b in range(a + 1, n_ens)]

    def back_copy(s, b, r, lon, to):
        return pltpu.make_async_remote_copy(
            src_ref=grads.at[s, to],
            dst_ref=out_ref.at[r, 0, :, pl.ds(pl.multiple_of(lon * LANE, LANE), LANE)],
            send_sem=back_send.at[s, to],
            recv_sem=back_recv.at[b],
            device_id=place(to, lat),
            device_id_type=MESH,
        )

    def self_copy(s, r, lon):
        return pltpu.make_async_copy(
            grads.at[s, me],
            out_ref.at[r, 0, :, pl.ds(pl.multiple_of(lon * LANE, LANE), LANE)],
            self_sem.at[s],
        )

    def score(s, b):
        r, lon = block_place(b)
        for k in range(1, n_ens):
            fwd_copy(s, me, ens_peer(k)).wait_recv()
        area = area_ref[first + r]

        def square(v, sums):
            rows = pl.ds(pl.multiple_of(v * 8, 8), 8)
            x = [recv[s, m, rows, :] for m in range(n_ens)]
            goal = target[s, rows, :]
            gaps = [xm - goal for xm in x] + [x[a] - x[c] for a, c in pairs]
            return tuple(total + gap * gap for total, gap in zip(sums, gaps))

        zero = jnp.zeros((8, LANE), F32)
        sums = lax.fori_loop(0, C // 8, square, (zero,) * (n_ens + len(pairs)))
        scaled = []
        skill_sum = jnp.zeros((1, LANE), F32)
        pair_sum = jnp.zeros((1, LANE), F32)
        for at, total in enumerate(sums):
            mean = jnp.sum(total, axis=0, keepdims=True) * (1.0 / C) + 1.0
            inverse = lax.rsqrt(mean)
            if at < n_ens:
                skill_sum = skill_sum + mean * inverse
                scaled.append(jnp.broadcast_to(inverse * area, (8, LANE)))
            else:
                pair_sum = pair_sum + mean * inverse
                scaled.append(jnp.broadcast_to(inverse * (area * (1.0 / n_ens)), (8, LANE)))
        cell = skill_sum * (1.0 / n_ens) - (2.0 * pair_sum + n_ens) * (1.0 / (2 * n_ens * n_ens))

        @pl.loop(0, C // 8)
        def _(v):
            rows = pl.ds(pl.multiple_of(v * 8, 8), 8)
            x = [recv[s, m, rows, :] for m in range(n_ens)]
            goal = target[s, rows, :]
            g = [(x[m] - goal) * scaled[m] for m in range(n_ens)]
            for at, (a, c) in enumerate(pairs):
                pull = (x[a] - x[c]) * scaled[n_ens + at]
                g[a] = g[a] - pull
                g[c] = g[c] + pull
            for m in range(n_ens):
                grads[s, m, rows, :] = g[m]

        for k in range(1, n_ens):
            back_copy(s, b, r, lon, ens_peer(k)).start()
        self_copy(s, r, lon).start()
        return jnp.broadcast_to(area * cell, (8, LANE))

    part = score(0, me)
    for s in range(1, slots):
        part = part + score(s, n_ens * s + me)
    lossbuf1[me] = part

    @pl.when(me == extra)
    def _():
        recv[slots, me] = states[BLOCKS - 1]
        lossbuf1[me] += score(slots, BLOCKS - 1)

    def level(buf, send, got, count, mine, peer):
        def copy(k, slot):
            return pltpu.make_async_remote_copy(
                src_ref=buf.at[mine],
                dst_ref=buf.at[slot],
                send_sem=send.at[k],
                recv_sem=got.at[slot],
                device_id=peer(k),
                device_id_type=MESH,
            )

        for k in range(1, count):
            copy(k, mine).start()
        for k in range(1, count):
            copy(k, lax.rem(mine + k, count)).wait_recv()
        total = buf[0]
        for k in range(1, count):
            total = total + buf[k]
        return total, lambda: [copy(k, mine).wait_send() for k in range(1, count)]

    total, done1 = level(lossbuf1, l1_send, l1_recv, n_ens, me, lambda k: place(ens_peer(k), lat))
    lossbuf2[inner] = total
    total, done2 = level(lossbuf2, l2_send, l2_recv, group, inner, lambda k: place(me, inner_peer(k)))
    lossbuf3[outer] = total
    total, done3 = level(lossbuf3, l3_send, l3_recv, tall, outer, lambda k: place(me, outer_peer(k)))
    loss_ref[0] = jnp.sum(total[0:1, :]) * (1.0 / (n_lat * ROWS * NLON))

    def wait_back(b, owner):
        @pl.when(me != owner)
        def _():
            r, lon = block_place(b)
            back_copy(0, b, r, lon, me).wait_recv()

    for s in range(slots):
        b = n_ens * s + me
        self_copy(s, *block_place(b)).wait()
        for k in range(1, n_ens):
            to = ens_peer(k)
            c = n_ens * s + to
            back_copy(s, c, *block_place(c), me).wait_recv()
            back_copy(s, b, *block_place(b), to).wait_send()
            fwd_copy(s, to, me).wait_send()
    last = BLOCKS - 1

    @pl.when(me == extra)
    def _():
        self_copy(slots, *block_place(last)).wait()
        for k in range(1, n_ens):
            back_copy(slots, last, *block_place(last), ens_peer(k)).wait_send()

    @pl.when(me != extra)
    def _():
        back_copy(slots, last, *block_place(last), me).wait_recv()
        fwd_copy(slots, extra, me).wait_send()

    for done in (done1, done2, done3):
        done()

    def sent(side, there):
        @pl.when(there)
        def _():
            for chunk in range(len(CHUNKS)):
                halo_copy(side, chunk).wait_send()

    sent(0, has_up)
    sent(1, has_down)


def area_weights(total_rows):
    latitude = (jnp.arange(total_rows, dtype=F32) + 0.5) * (math.pi / total_rows) - 0.5 * math.pi
    cosine = jnp.cos(latitude)
    return cosine / jnp.mean(cosine)


def per_device(n_ens, n_lat, members, truth, target_time, row_taps, filters, mixing):
    taps = row_taps.reshape(ROWS * TAPS)
    spread = jnp.transpose(filters[0], (0, 3, 2, 1)).reshape(1, ROWS, LW, K, TAPS)[0]
    spread = jnp.pad(spread, ((0, 0), (0, 0), (0, KP - K), (0, 0))).reshape(ROWS, LW * KP, TAPS)
    mix = jnp.transpose(mixing[0], (1, 0, 2))
    area = area_weights(n_lat * ROWS)
    slots = BLOCKS // n_ens
    group = min(8, n_lat)
    tall = n_lat // group
    vmem = pltpu.VMEM
    dma = pltpu.SemaphoreType.DMA
    smem_spec = pl.BlockSpec(memory_space=pltpu.SMEM)
    vmem_spec = pl.BlockSpec(memory_space=pltpu.VMEM)
    any_spec = pl.BlockSpec(memory_space=pl.ANY)
    return pl.pallas_call(
        functools.partial(kernel, n_ens, n_lat),
        out_shape=(
            jax.ShapeDtypeStruct((ROWS, 1, C, NLON), F32),
            jax.ShapeDtypeStruct((1,), F32),
        ),
        in_specs=[smem_spec, smem_spec, smem_spec, vmem_spec, vmem_spec, any_spec, any_spec],
        out_specs=(any_spec, smem_spec),
        scratch_shapes=[
            vmem((ROWS, C, NLON), F32),
            vmem((2, REACH, C, NLON), F32),
            vmem((OWN_PAD, NLON), BF16),
            vmem((OWN_PAD, NLON), BF16),
            vmem((SIDE, NLON), BF16),
            vmem((SIDE, NLON), BF16),
            vmem((K, C, LANE), F32),
            vmem((ROWS * LW, KP, OWN_PAD), F32),
            vmem((2, ROWS * LW, KP, SIDE), F32),
            vmem((ROWS * BAND, OWN_PAD), BF16),
            vmem((ROWS * BAND, OWN_PAD), BF16),
            vmem((REACH * BAND, SIDE), BF16),
            vmem((REACH * BAND, SIDE), BF16),
            vmem((ROWS * BAND, NLON), F32),
            vmem((BLOCKS, C, LANE), F32),
            vmem((slots + 1, n_ens, C, LANE), F32),
            vmem((slots + 1, n_ens, C, LANE), F32),
            vmem((slots + 1, 4, C, LANE), F32),
            vmem((slots + 1, C, LANE), F32),
            vmem((n_ens, 8, LANE), F32),
            vmem((group, 8, LANE), F32),
            vmem((tall, 8, LANE), F32),
            dma,
            dma((slots + 1,)),
            dma((2, len(CHUNKS))),
            dma((2, len(CHUNKS))),
            dma((slots + 1, n_ens)),
            dma((slots + 1, n_ens)),
            dma((slots + 1, n_ens)),
            dma((BLOCKS,)),
            dma((slots + 1,)),
            dma((n_ens,)),
            dma((n_ens,)),
            dma((group,)),
            dma((group,)),
            dma((tall,)),
            dma((tall,)),
        ],
        compiler_params=pltpu.CompilerParams(
            collective_id=0, has_side_effects=True, vmem_limit_bytes=60 * 2**20
        ),
        cost_estimate=pl.CostEstimate(flops=5_000_000_000, bytes_accessed=4_000_000, transcendentals=400_000),
    )(taps, target_time, area, spread, mix, members, truth)


def solution(mesh):
    placed = (
        P("lat", "ens", None, None),
        P(None, "lat", None, None),
        P("lat"),
        P(None, "lat", None),
        P(None, "lat", None, None, None),
        P(),
    )
    return jax.shard_map(
        functools.partial(per_device, mesh.shape["ens"], mesh.shape["lat"]),
        mesh=mesh,
        in_specs=placed,
        out_specs=(P("lat", "ens", None, None), P()),
        check_vma=False,
    )
```

```python
import functools
import math

import jax
import jax.numpy as jnp
import numpy as np
from jax import lax
from jax.experimental import pallas as pl
from jax.experimental.pallas import tpu as pltpu
from jax.sharding import PartitionSpec as P

C = 64
NLON = 640
K = 9
KP = 16
TAPS = 5
LW = 5
REACH = 4
ROWS = 5
LANE = 128
NB = NLON // LANE
BLOCKS = ROWS * NB
SIDE = REACH * C
OWN = ROWS * C
OWN_PAD = 384
BAND = LW * C
MESH = pl.DeviceIdType.MESH
CHUNKS = ((0, 256), (256, 256), (512, 128))
F32 = jnp.float32
BF16 = jnp.bfloat16


def split(x):
    hi = x.astype(BF16)
    return hi, (x - hi.astype(F32)).astype(BF16)


def dot3(w_hi, w_lo, x_hi, x_lo):
    dot = functools.partial(jnp.dot, preferred_element_type=F32)
    return dot(w_hi, x_hi) + dot(w_hi, x_lo) + dot(w_lo, x_hi)


def block_place(b):
    return lax.rem(b, ROWS), lax.rem(b // ROWS + 1, NB)


def kernel(
    n_ens,
    n_lat,
    taps_ref,
    time_ref,
    area_ref,
    filt_ref,
    mix_ref,
    members_ref,
    truth_ref,
    out_ref,
    loss_ref,
    own,
    halo,
    own_hi,
    own_lo,
    side_hi,
    side_lo,
    rows_in,
    mdup,
    a_own,
    a_side,
    w_own_hi,
    w_own_lo,
    w_side_hi,
    w_side_lo,
    acc,
    states,
    recv,
    grads,
    cand,
    target,
    lossbuf1,
    lossbuf2,
    lossbuf3,
    own_sem,
    cand_sem,
    halo_send,
    halo_recv,
    fwd_send,
    fwd_recv,
    back_send,
    back_recv,
    self_sem,
    l1_send,
    l1_recv,
    l2_send,
    l2_recv,
    l3_send,
    l3_recv,
):
    me = lax.axis_index("ens")
    lat = lax.axis_index("lat")
    group = min(8, n_lat)
    tall = n_lat // group
    first = lat * ROWS
    core = lax.rem(lat, 2)
    near = 1 - core
    far = core
    slots = BLOCKS // n_ens
    extra = lax.rem(core * (n_ens // 2) + lax.rem(lat // 2, n_ens // 2), n_ens)
    inner = lax.rem(lat, group)
    outer = lat // group
    has_up = lat < n_lat - 1
    has_down = lat > 0

    def place(ens_at, lat_at):
        return {"ens": ens_at, "lat": lat_at}

    def ens_peer(k):
        return lax.rem(me + k, n_ens)

    def inner_peer(k):
        return outer * group + lax.rem(inner + k, group)

    def outer_peer(k):
        return lax.rem(outer + k, tall) * group + inner

    own_copy = pltpu.make_async_copy(members_ref.at[:, 0], own, own_sem)
    own_copy.start()

    def cand_copy(s):
        r, lon = block_place(n_ens * s + me)
        return pltpu.make_async_copy(
            truth_ref.at[:, r, :, pl.ds(pl.multiple_of(lon * LANE, LANE), LANE)], cand.at[s], cand_sem.at[s]
        )

    for s in range(slots):
        cand_copy(s).start()

    @pl.when(me == extra)
    def _():
        r, lon = ROWS - 1, 0
        pltpu.make_async_copy(truth_ref.at[:, r, :, pl.ds(lon, LANE)], cand.at[slots], cand_sem.at[slots]).start()

    barrier = pltpu.get_barrier_semaphore()
    for k in range(1, n_ens):
        pl.semaphore_signal(barrier, inc=1, device_id=place(ens_peer(k), lat), device_id_type=MESH)
    for k in range(1, group):
        pl.semaphore_signal(barrier, inc=1, device_id=place(me, inner_peer(k)), device_id_type=MESH)
    for k in range(1, tall):
        pl.semaphore_signal(barrier, inc=1, device_id=place(me, outer_peer(k)), device_id_type=MESH)
    over_up = has_up & (inner == group - 1)
    over_down = has_down & (inner == 0)

    @pl.when(over_up)
    def _():
        pl.semaphore_signal(barrier, inc=1, device_id=place(me, lat + 1), device_id_type=MESH)

    @pl.when(over_down)
    def _():
        pl.semaphore_signal(barrier, inc=1, device_id=place(me, lat - 1), device_id_type=MESH)

    greeted = n_ens - 1 + group - 1 + tall - 1
    pl.semaphore_wait(barrier, greeted + over_up.astype(jnp.int32) + over_down.astype(jnp.int32))

    def halo_copy(side, chunk):
        start, width = CHUNKS[chunk]
        rows = pl.ds(1, REACH) if side == 0 else pl.ds(0, REACH)
        to = lat + 1 if side == 0 else lat - 1
        return pltpu.make_async_remote_copy(
            src_ref=members_ref.at[rows, 0, :, pl.ds(start, width)],
            dst_ref=halo.at[side, :, :, pl.ds(start, width)],
            send_sem=halo_send.at[side, chunk],
            recv_sem=halo_recv.at[side, chunk],
            device_id=place(me, to),
            device_id_type=MESH,
        )

    def send_side(side):
        for chunk in range(len(CHUNKS)):
            halo_copy(side, chunk).start()

    @pl.when((core == 1) & has_up)
    def _():
        send_side(0)

    @pl.when((core == 0) & has_down)
    def _():
        send_side(1)

    @pl.when((core == 0) & has_up)
    def _():
        send_side(0)

    @pl.when((core == 1) & has_down)
    def _():
        send_side(1)

    @pl.when(jnp.logical_not(has_down))
    def _():
        halo[0] = jnp.zeros_like(halo[0])

    @pl.when(jnp.logical_not(has_up))
    def _():
        halo[1] = jnp.zeros_like(halo[1])

    for k in range(K):
        mdup[k] = jnp.concatenate([mix_ref[k], mix_ref[k]], axis=1)

    def row_of(width, low, high):
        lane = lax.broadcasted_iota(jnp.int32, (1, width), 1)
        q = low + lane // C
        return jnp.where(q < high, q, -1)

    q_own = row_of(OWN_PAD, REACH, REACH + ROWS)
    q_sides = (row_of(SIDE, 0, REACH), row_of(SIDE, REACH + ROWS, ROWS + 2 * REACH))

    for i in range(ROWS * TAPS * LW):
        rows_in[i : i + 1, :K] = filt_ref[i]
    turned = jnp.transpose(rows_in[...])[:KP]

    for r in range(ROWS):
        hits = [
            [(q == taps_ref[r, 0, t] - first + REACH).astype(F32) for t in range(TAPS)] for q in (q_own, *q_sides)
        ]
        for d in range(LW):
            columns = [(r * TAPS + t) * LW + d for t in range(TAPS)]
            columns = [jnp.broadcast_to(turned[:, at : at + 1], (KP, LANE)) for at in columns]
            for ref, hit in zip((a_own, a_side.at[0], a_side.at[1]), hits):
                for at in range(0, ref.shape[2], LANE):
                    terms = [columns[t] * hit[t][:, at : at + LANE] for t in range(TAPS)]
                    ref[r * LW + d, :, at : at + LANE] = functools.reduce(jnp.add, terms)

    def weights(rd, a_at, width):
        for at in range(0, width, LANE):
            total = None
            for k in range(K):
                term = a_at[rd, k : k + 1, at : at + LANE] * mdup[k]
                total = term if total is None else total + term
            yield at, split(total)

    @pl.loop(0, ROWS * LW)
    def _(rd):
        rows = pl.ds(pl.multiple_of(rd * C, C), C)
        for at, (hi, lo) in weights(rd, a_own, OWN_PAD):
            w_own_hi[rows, at : at + LANE] = hi
            w_own_lo[rows, at : at + LANE] = lo

    own_copy.wait()
    hi, lo = split(own[...].reshape(OWN, NLON))
    own_hi[:OWN] = hi
    own_lo[:OWN] = lo
    own_hi[OWN:] = jnp.zeros((OWN_PAD - OWN, NLON), BF16)
    own_lo[OWN:] = jnp.zeros((OWN_PAD - OWN, NLON), BF16)

    @pl.loop(0, ROWS)
    def _(r):
        rows = pl.ds(pl.multiple_of(r * BAND, BAND), BAND)
        for start, width in CHUNKS:
            lons = pl.ds(start, width)
            acc[rows, lons] = dot3(w_own_hi[rows, :], w_own_lo[rows, :], own_hi[:, lons], own_lo[:, lons])

    def side_weights(side):
        a_at = a_side.at[side]

        @pl.loop(0, REACH * LW)
        def _(i):
            rows = pl.ds(pl.multiple_of(i * C, C), C)
            for at, (hi, lo) in weights(i + side * LW, a_at, SIDE):
                w_side_hi[rows, at : at + LANE] = hi
                w_side_lo[rows, at : at + LANE] = lo

    def wait_halo(side, chunk):
        @pl.when((side == 0) & has_down)
        def _():
            halo_copy(0, chunk).wait_recv()

        @pl.when((side == 1) & has_up)
        def _():
            halo_copy(1, chunk).wait_recv()

    def add_side(side, chunk):
        start, width = CHUNKS[chunk]
        lons = pl.ds(start, width)
        hi, lo = split(halo[side, :, :, lons].reshape(SIDE, width))
        side_hi[:, lons] = hi
        side_lo[:, lons] = lo

        @pl.loop(0, REACH)
        def _(i):
            rows = pl.ds(pl.multiple_of(i * BAND, BAND), BAND)
            acc_rows = pl.ds(pl.multiple_of((i + side) * BAND, BAND), BAND)
            acc[acc_rows, lons] += dot3(w_side_hi[rows, :], w_side_lo[rows, :], side_hi[:, lons], side_lo[:, lons])

    side_weights(near)
    for chunk in range(len(CHUNKS)):
        wait_halo(near, chunk)
        add_side(near, chunk)
    side_weights(far)

    def pick_target(s, r):
        time = time_ref[r]
        picked = cand[s, 0]
        for t in range(1, 4):
            picked = jnp.where(time == t, cand[s, t], picked)
        target[s] = picked

    for s in range(slots):
        cand_copy(s).wait()
        pick_target(s, lax.rem(n_ens * s + me, ROWS))

    @pl.when(me == extra)
    def _():
        pltpu.make_async_copy(truth_ref.at[:, ROWS - 1, :, pl.ds(0, LANE)], cand.at[slots], cand_sem.at[slots]).wait()
        pick_target(slots, ROWS - 1)

    lane = lax.broadcasted_iota(jnp.int32, (C, LANE), 1)

    def finish(lon, first_block):
        @pl.loop(0, ROWS)
        def _(r):
            def part(d, at):
                rows = pl.ds(pl.multiple_of(r * BAND + d * C, C), C)
                return acc[rows, at * LANE : (at + 1) * LANE]

            total = part(2, lon)
            for d in (0, 1, 3, 4):
                shift = d - LW // 2
                if shift > 0:
                    mine = jnp.where(lane < shift, part(d, (lon + 1) % NB), part(d, lon))
                else:
                    mine = jnp.where(lane >= LANE + shift, part(d, (lon - 1) % NB), part(d, lon))
                total = total + pltpu.roll(mine, (-shift) % LANE, 1)
            cube = total + 0.044715 * total * total * total
            gelu = 0.5 * total * (1.0 + jnp.tanh(math.sqrt(2.0 / math.pi) * cube))
            states[first_block + r] = own[r, :, lon * LANE : (lon + 1) * LANE] + gelu

    def fwd_copy(s, to, source):
        return pltpu.make_async_remote_copy(
            src_ref=states.at[n_ens * s + to] if s < slots else states.at[BLOCKS - 1],
            dst_ref=recv.at[s, source],
            send_sem=fwd_send.at[s, to],
            recv_sem=fwd_recv.at[s, source],
            device_id=place(to, lat),
            device_id_type=MESH,
        )

    def send_slot(s):
        for k in range(1, n_ens):
            fwd_copy(s, ens_peer(k), me).start()
        recv[s, me] = states[n_ens * s + me]

    for chunk in (0, 1):
        wait_halo(far, chunk)
        add_side(far, chunk)
    finish(1, 0)
    finish(2, 5)
    send_slot(0)
    wait_halo(far, 2)
    add_side(far, 2)
    finish(3, 10)
    for s in range(1, slots):
        if n_ens * (s + 1) <= 15:
            send_slot(s)
    finish(4, 15)
    finish(0, 20)
    for s in range(1, slots):
        if n_ens * (s + 1) > 15:
            send_slot(s)

    @pl.when(me != extra)
    def _():
        fwd_copy(slots, extra, me).start()

    pairs = [(a, b) for a in range(n_ens) for b in range(a + 1, n_ens)]

    def back_copy(s, b, r, lon, to):
        return pltpu.make_async_remote_copy(
            src_ref=grads.at[s, to],
            dst_ref=out_ref.at[r, 0, :, pl.ds(pl.multiple_of(lon * LANE, LANE), LANE)],
            send_sem=back_send.at[s, to],
            recv_sem=back_recv.at[b],
            device_id=place(to, lat),
            device_id_type=MESH,
        )

    def self_copy(s, r, lon):
        return pltpu.make_async_copy(
            grads.at[s, me],
            out_ref.at[r, 0, :, pl.ds(pl.multiple_of(lon * LANE, LANE), LANE)],
            self_sem.at[s],
        )

    def score(s, b):
        r, lon = block_place(b)
        for k in range(1, n_ens):
            fwd_copy(s, me, ens_peer(k)).wait_recv()
        area = area_ref[first + r]

        def square(v, sums):
            rows = pl.ds(pl.multiple_of(v * 8, 8), 8)
            x = [recv[s, m, rows, :] for m in range(n_ens)]
            goal = target[s, rows, :]
            gaps = [xm - goal for xm in x] + [x[a] - x[c] for a, c in pairs]
            return tuple(total + gap * gap for total, gap in zip(sums, gaps))

        zero = jnp.zeros((8, LANE), F32)
        sums = lax.fori_loop(0, C // 8, square, (zero,) * (n_ens + len(pairs)))
        scaled = []
        skill_sum = jnp.zeros((1, LANE), F32)
        pair_sum = jnp.zeros((1, LANE), F32)
        for at, total in enumerate(sums):
            mean = jnp.sum(total, axis=0, keepdims=True) * (1.0 / C) + 1.0
            inverse = lax.rsqrt(mean)
            if at < n_ens:
                skill_sum = skill_sum + mean * inverse
                scaled.append(jnp.broadcast_to(inverse * area, (8, LANE)))
            else:
                pair_sum = pair_sum + mean * inverse
                scaled.append(jnp.broadcast_to(inverse * (area * (1.0 / n_ens)), (8, LANE)))
        cell = skill_sum * (1.0 / n_ens) - (2.0 * pair_sum + n_ens) * (1.0 / (2 * n_ens * n_ens))

        @pl.loop(0, C // 8)
        def _(v):
            rows = pl.ds(pl.multiple_of(v * 8, 8), 8)
            x = [recv[s, m, rows, :] for m in range(n_ens)]
            goal = target[s, rows, :]
            g = [(x[m] - goal) * scaled[m] for m in range(n_ens)]
            for at, (a, c) in enumerate(pairs):
                pull = (x[a] - x[c]) * scaled[n_ens + at]
                g[a] = g[a] - pull
                g[c] = g[c] + pull
            for m in range(n_ens):
                grads[s, m, rows, :] = g[m]

        for k in range(1, n_ens):
            back_copy(s, b, r, lon, ens_peer(k)).start()
        self_copy(s, r, lon).start()
        return jnp.broadcast_to(area * cell, (8, LANE))

    part = score(0, me)
    for s in range(1, slots):
        part = part + score(s, n_ens * s + me)
    lossbuf1[me] = part

    @pl.when(me == extra)
    def _():
        recv[slots, me] = states[BLOCKS - 1]
        lossbuf1[me] += score(slots, BLOCKS - 1)

    def level(buf, send, got, count, mine, peer):
        def copy(k, slot):
            return pltpu.make_async_remote_copy(
                src_ref=buf.at[mine],
                dst_ref=buf.at[slot],
                send_sem=send.at[k],
                recv_sem=got.at[slot],
                device_id=peer(k),
                device_id_type=MESH,
            )

        for k in range(1, count):
            copy(k, mine).start()
        for k in range(1, count):
            copy(k, lax.rem(mine + k, count)).wait_recv()
        total = buf[0]
        for k in range(1, count):
            total = total + buf[k]
        return total, lambda: [copy(k, mine).wait_send() for k in range(1, count)]

    total, done1 = level(lossbuf1, l1_send, l1_recv, n_ens, me, lambda k: place(ens_peer(k), lat))
    lossbuf2[inner] = total
    total, done2 = level(lossbuf2, l2_send, l2_recv, group, inner, lambda k: place(me, inner_peer(k)))
    lossbuf3[outer] = total
    total, done3 = level(lossbuf3, l3_send, l3_recv, tall, outer, lambda k: place(me, outer_peer(k)))
    loss_ref[0] = jnp.sum(total[0:1, :]) * (1.0 / (n_lat * ROWS * NLON))

    def wait_back(b, owner):
        @pl.when(me != owner)
        def _():
            r, lon = block_place(b)
            back_copy(0, b, r, lon, me).wait_recv()

    for s in range(slots):
        b = n_ens * s + me
        self_copy(s, *block_place(b)).wait()
        for k in range(1, n_ens):
            to = ens_peer(k)
            c = n_ens * s + to
            back_copy(s, c, *block_place(c), me).wait_recv()
            back_copy(s, b, *block_place(b), to).wait_send()
            fwd_copy(s, to, me).wait_send()
    last = BLOCKS - 1

    @pl.when(me == extra)
    def _():
        self_copy(slots, *block_place(last)).wait()
        for k in range(1, n_ens):
            back_copy(slots, last, *block_place(last), ens_peer(k)).wait_send()

    @pl.when(me != extra)
    def _():
        back_copy(slots, last, *block_place(last), me).wait_recv()
        fwd_copy(slots, extra, me).wait_send()

    for done in (done1, done2, done3):
        done()

    def sent(side, there):
        @pl.when(there)
        def _():
            for chunk in range(len(CHUNKS)):
                halo_copy(side, chunk).wait_send()

    sent(0, has_up)
    sent(1, has_down)


def area_weights(total_rows):
    latitude = (np.arange(total_rows, dtype=np.float64) + 0.5) * (math.pi / total_rows) - 0.5 * math.pi
    cosine = np.cos(latitude)
    return (cosine / np.mean(cosine)).astype(np.float32)


def per_device(n_ens, n_lat, members, truth, target_time, row_taps, filters, mixing):
    taps = jnp.transpose(row_taps, (1, 0, 2))
    spread = jnp.transpose(filters, (1, 2, 4, 0, 3)).reshape(ROWS * TAPS * LW, 1, K)
    mix = jnp.transpose(mixing[0], (1, 0, 2))
    area = jnp.asarray(area_weights(n_lat * ROWS))
    slots = BLOCKS // n_ens
    group = min(8, n_lat)
    tall = n_lat // group
    vmem = pltpu.VMEM
    dma = pltpu.SemaphoreType.DMA
    smem_spec = pl.BlockSpec(memory_space=pltpu.SMEM)
    vmem_spec = pl.BlockSpec(memory_space=pltpu.VMEM)
    any_spec = pl.BlockSpec(memory_space=pl.ANY)
    hbm_spec = pl.BlockSpec(memory_space=pltpu.HBM)
    return pl.pallas_call(
        functools.partial(kernel, n_ens, n_lat),
        out_shape=(
            jax.ShapeDtypeStruct((ROWS, 1, C, NLON), F32),
            jax.ShapeDtypeStruct((1,), F32),
        ),
        in_specs=[smem_spec, smem_spec, smem_spec, vmem_spec, vmem_spec, hbm_spec, hbm_spec],
        out_specs=(any_spec, smem_spec),
        scratch_shapes=[
            vmem((ROWS, C, NLON), F32),
            vmem((2, REACH, C, NLON), F32),
            vmem((OWN_PAD, NLON), BF16),
            vmem((OWN_PAD, NLON), BF16),
            vmem((SIDE, NLON), BF16),
            vmem((SIDE, NLON), BF16),
            vmem((LANE, LANE), F32),
            vmem((K, C, LANE), F32),
            vmem((ROWS * LW, KP, OWN_PAD), F32),
            vmem((2, ROWS * LW, KP, SIDE), F32),
            vmem((ROWS * BAND, OWN_PAD), BF16),
            vmem((ROWS * BAND, OWN_PAD), BF16),
            vmem((REACH * BAND, SIDE), BF16),
            vmem((REACH * BAND, SIDE), BF16),
            vmem((ROWS * BAND, NLON), F32),
            vmem((BLOCKS, C, LANE), F32),
            vmem((slots + 1, n_ens, C, LANE), F32),
            vmem((slots + 1, n_ens, C, LANE), F32),
            vmem((slots + 1, 4, C, LANE), F32),
            vmem((slots + 1, C, LANE), F32),
            vmem((n_ens, 8, LANE), F32),
            vmem((group, 8, LANE), F32),
            vmem((tall, 8, LANE), F32),
            dma,
            dma((slots + 1,)),
            dma((2, len(CHUNKS))),
            dma((2, len(CHUNKS))),
            dma((slots + 1, n_ens)),
            dma((slots + 1, n_ens)),
            dma((slots + 1, n_ens)),
            dma((BLOCKS,)),
            dma((slots + 1,)),
            dma((n_ens,)),
            dma((n_ens,)),
            dma((group,)),
            dma((group,)),
            dma((tall,)),
            dma((tall,)),
        ],
        compiler_params=pltpu.CompilerParams(
            collective_id=0, has_side_effects=True, vmem_limit_bytes=58 * 2**20
        ),
        cost_estimate=pl.CostEstimate(flops=5_000_000_000, bytes_accessed=4_000_000, transcendentals=400_000),
    )(taps, target_time, area, spread, mix, members, truth)


def solution(mesh):
    placed = (
        P("lat", "ens", None, None),
        P(None, "lat", None, None),
        P("lat"),
        P(None, "lat", None),
        P(None, "lat", None, None, None),
        P(),
    )
    return jax.shard_map(
        functools.partial(per_device, mesh.shape["ens"], mesh.shape["lat"]),
        mesh=mesh,
        in_specs=placed,
        out_specs=(P("lat", "ens", None, None), P()),
        check_vma=False,
    )
```

```python
import functools
import math

import jax
import jax.numpy as jnp
import numpy as np
from jax import lax
from jax.experimental import pallas as pl
from jax.experimental.pallas import tpu as pltpu
from jax.sharding import PartitionSpec as P

C = 64
NLON = 640
K = 9
KP = 16
TAPS = 5
LW = 5
REACH = 4
ROWS = 5
LANE = 128
NB = NLON // LANE
BLOCKS = ROWS * NB
SIDE = REACH * C
OWN = ROWS * C
OWN_PAD = 384
BAND = LW * C
MESH = pl.DeviceIdType.MESH
CHUNKS = ((0, 256), (256, 256), (512, 128))
F32 = jnp.float32
BF16 = jnp.bfloat16


def split(x):
    hi = x.astype(BF16)
    return hi, (x - hi.astype(F32)).astype(BF16)


def dot3(w_hi, w_lo, x_hi, x_lo):
    dot = functools.partial(jnp.dot, preferred_element_type=F32)
    return dot(w_hi, x_hi) + dot(w_hi, x_lo) + dot(w_lo, x_hi)


def block_place(b):
    return lax.rem(b, ROWS), lax.rem(b // ROWS + 1, NB)


def kernel(
    n_ens,
    n_lat,
    taps_hbm,
    time_hbm,
    area_hbm,
    filt_hbm,
    mix_hbm,
    members_ref,
    truth_ref,
    out_ref,
    loss_ref,
    taps_ref,
    time_ref,
    area_ref,
    filt_ref,
    mix_ref,
    own,
    halo,
    own_hi,
    own_lo,
    side_hi,
    side_lo,
    rows_in,
    mdup,
    a_own,
    a_side,
    w_own_hi,
    w_own_lo,
    w_side_hi,
    w_side_lo,
    acc,
    states,
    recv,
    grads,
    cand,
    target,
    pulls,
    lossbuf1,
    lossbuf2,
    lossbuf3,
    small_sem,
    own_sem,
    cand_sem,
    halo_send,
    halo_recv,
    fwd_send,
    fwd_recv,
    back_send,
    back_recv,
    self_sem,
    l1_send,
    l1_recv,
    l2_send,
    l2_recv,
    l3_send,
    l3_recv,
):
    me = lax.axis_index("ens")
    lat = lax.axis_index("lat")
    group = min(8, n_lat)
    tall = n_lat // group
    first = lat * ROWS
    core = lax.rem(lat, 2)
    near = 1 - core
    far = core
    slots = BLOCKS // n_ens
    extra = lax.rem(core * (n_ens // 2) + lax.rem(lat // 2, n_ens // 2), n_ens)
    inner = lax.rem(lat, group)
    outer = lat // group
    has_up = lat < n_lat - 1
    has_down = lat > 0

    def place(ens_at, lat_at):
        return {"ens": ens_at, "lat": lat_at}

    def ens_peer(k):
        return lax.rem(me + k, n_ens)

    def inner_peer(k):
        return outer * group + lax.rem(inner + k, group)

    def outer_peer(k):
        return lax.rem(outer + k, tall) * group + inner

    barrier = pltpu.get_barrier_semaphore()
    for k in range(1, n_ens):
        pl.semaphore_signal(barrier, inc=1, device_id=place(ens_peer(k), lat), device_id_type=MESH)
    for k in range(1, group):
        pl.semaphore_signal(barrier, inc=1, device_id=place(me, inner_peer(k)), device_id_type=MESH)
    for k in range(1, tall):
        pl.semaphore_signal(barrier, inc=1, device_id=place(me, outer_peer(k)), device_id_type=MESH)
    over_up = has_up & (inner == group - 1)
    over_down = has_down & (inner == 0)

    @pl.when(over_up)
    def _():
        pl.semaphore_signal(barrier, inc=1, device_id=place(me, lat + 1), device_id_type=MESH)

    @pl.when(over_down)
    def _():
        pl.semaphore_signal(barrier, inc=1, device_id=place(me, lat - 1), device_id_type=MESH)

    smalls = [
        pltpu.make_async_copy(source, kept, small_sem.at[at])
        for at, (source, kept) in enumerate(
            (
                (mix_hbm, mix_ref),
                (filt_hbm, filt_ref),
                (taps_hbm, taps_ref),
                (time_hbm, time_ref),
                (area_hbm, area_ref),
            )
        )
    ]
    for small in smalls:
        small.start()
    own_copy = pltpu.make_async_copy(members_ref.at[:, 0], own, own_sem)
    own_copy.start()

    def cand_copy(s):
        r, lon = block_place(n_ens * s + me)
        return pltpu.make_async_copy(
            truth_ref.at[:, r, :, pl.ds(pl.multiple_of(lon * LANE, LANE), LANE)], cand.at[s], cand_sem.at[s]
        )

    for s in range(slots):
        cand_copy(s).start()

    @pl.when(me == extra)
    def _():
        r, lon = ROWS - 1, 0
        pltpu.make_async_copy(truth_ref.at[:, r, :, pl.ds(lon, LANE)], cand.at[slots], cand_sem.at[slots]).start()

    greeted = n_ens - 1 + group - 1 + tall - 1
    pl.semaphore_wait(barrier, greeted + over_up.astype(jnp.int32) + over_down.astype(jnp.int32))

    def halo_copy(side, chunk):
        start, width = CHUNKS[chunk]
        rows = pl.ds(1, REACH) if side == 0 else pl.ds(0, REACH)
        to = lat + 1 if side == 0 else lat - 1
        return pltpu.make_async_remote_copy(
            src_ref=members_ref.at[rows, 0, :, pl.ds(start, width)],
            dst_ref=halo.at[side, :, :, pl.ds(start, width)],
            send_sem=halo_send.at[side, chunk],
            recv_sem=halo_recv.at[side, chunk],
            device_id=place(me, to),
            device_id_type=MESH,
        )

    def send_side(side):
        for chunk in range(len(CHUNKS)):
            halo_copy(side, chunk).start()

    @pl.when((core == 1) & has_up)
    def _():
        send_side(0)

    @pl.when((core == 0) & has_down)
    def _():
        send_side(1)

    @pl.when((core == 0) & has_up)
    def _():
        send_side(0)

    @pl.when((core == 1) & has_down)
    def _():
        send_side(1)

    @pl.when(jnp.logical_not(has_down))
    def _():
        halo[0] = jnp.zeros_like(halo[0])

    @pl.when(jnp.logical_not(has_up))
    def _():
        halo[1] = jnp.zeros_like(halo[1])

    for small in smalls:
        small.wait()

    for k in range(K):
        mdup[k] = jnp.concatenate([mix_ref[k], mix_ref[k]], axis=1)

    def row_of(width, low, high):
        lane = lax.broadcasted_iota(jnp.int32, (1, width), 1)
        q = low + lane // C
        return jnp.where(q < high, q, -1)

    q_own = row_of(OWN_PAD, REACH, REACH + ROWS)
    q_sides = (row_of(SIDE, 0, REACH), row_of(SIDE, REACH + ROWS, ROWS + 2 * REACH))

    for i in range(ROWS * TAPS * LW):
        rows_in[i : i + 1, :K] = filt_ref[i]
    turned = jnp.transpose(rows_in[...])[:KP]

    for r in range(ROWS):
        hits = [
            [(q == taps_ref[r, 0, t] - first + REACH).astype(F32) for t in range(TAPS)] for q in (q_own, *q_sides)
        ]
        for d in range(LW):
            columns = [(r * TAPS + t) * LW + d for t in range(TAPS)]
            columns = [jnp.broadcast_to(turned[:, at : at + 1], (KP, LANE)) for at in columns]
            for ref, hit in zip((a_own, a_side.at[0], a_side.at[1]), hits):
                for at in range(0, ref.shape[2], LANE):
                    terms = [columns[t] * hit[t][:, at : at + LANE] for t in range(TAPS)]
                    ref[r * LW + d, :, at : at + LANE] = functools.reduce(jnp.add, terms)

    def weights(rd, a_at, width):
        for at in range(0, width, LANE):
            total = None
            for k in range(K):
                term = a_at[rd, k : k + 1, at : at + LANE] * mdup[k]
                total = term if total is None else total + term
            yield at, split(total)

    @pl.loop(0, ROWS * LW)
    def _(rd):
        rows = pl.ds(pl.multiple_of(rd * C, C), C)
        for at, (hi, lo) in weights(rd, a_own, OWN_PAD):
            w_own_hi[rows, at : at + LANE] = hi
            w_own_lo[rows, at : at + LANE] = lo

    own_copy.wait()
    hi, lo = split(own[...].reshape(OWN, NLON))
    own_hi[:OWN] = hi
    own_lo[:OWN] = lo
    own_hi[OWN:] = jnp.zeros((OWN_PAD - OWN, NLON), BF16)
    own_lo[OWN:] = jnp.zeros((OWN_PAD - OWN, NLON), BF16)

    @pl.loop(0, ROWS)
    def _(r):
        rows = pl.ds(pl.multiple_of(r * BAND, BAND), BAND)
        for start, width in CHUNKS:
            lons = pl.ds(start, width)
            acc[rows, lons] = dot3(w_own_hi[rows, :], w_own_lo[rows, :], own_hi[:, lons], own_lo[:, lons])

    def side_weights(side):
        a_at = a_side.at[side]

        @pl.loop(0, REACH * LW)
        def _(i):
            rows = pl.ds(pl.multiple_of(i * C, C), C)
            for at, (hi, lo) in weights(i + side * LW, a_at, SIDE):
                w_side_hi[rows, at : at + LANE] = hi
                w_side_lo[rows, at : at + LANE] = lo

    def wait_halo(side, chunk):
        @pl.when((side == 0) & has_down)
        def _():
            halo_copy(0, chunk).wait_recv()

        @pl.when((side == 1) & has_up)
        def _():
            halo_copy(1, chunk).wait_recv()

    def add_side(side, chunk):
        start, width = CHUNKS[chunk]
        lons = pl.ds(start, width)
        hi, lo = split(halo[side, :, :, lons].reshape(SIDE, width))
        side_hi[:, lons] = hi
        side_lo[:, lons] = lo

        @pl.loop(0, REACH)
        def _(i):
            rows = pl.ds(pl.multiple_of(i * BAND, BAND), BAND)
            acc_rows = pl.ds(pl.multiple_of((i + side) * BAND, BAND), BAND)
            acc[acc_rows, lons] += dot3(w_side_hi[rows, :], w_side_lo[rows, :], side_hi[:, lons], side_lo[:, lons])

    side_weights(near)
    for chunk in range(len(CHUNKS)):
        wait_halo(near, chunk)
        add_side(near, chunk)
    side_weights(far)

    def pick_target(s, r):
        time = time_ref[r]
        picked = cand[s, 0]
        for t in range(1, 4):
            picked = jnp.where(time == t, cand[s, t], picked)
        target[s] = picked

    for s in range(slots):
        cand_copy(s).wait()
        pick_target(s, lax.rem(n_ens * s + me, ROWS))

    @pl.when(me == extra)
    def _():
        pltpu.make_async_copy(truth_ref.at[:, ROWS - 1, :, pl.ds(0, LANE)], cand.at[slots], cand_sem.at[slots]).wait()
        pick_target(slots, ROWS - 1)

    lane = lax.broadcasted_iota(jnp.int32, (C, LANE), 1)

    def finish(lon, first_block):
        @pl.loop(0, ROWS)
        def _(r):
            def part(d, at):
                rows = pl.ds(pl.multiple_of(r * BAND + d * C, C), C)
                return acc[rows, at * LANE : (at + 1) * LANE]

            total = part(2, lon)
            for d in (0, 1, 3, 4):
                shift = d - LW // 2
                if shift > 0:
                    mine = jnp.where(lane < shift, part(d, (lon + 1) % NB), part(d, lon))
                else:
                    mine = jnp.where(lane >= LANE + shift, part(d, (lon - 1) % NB), part(d, lon))
                total = total + pltpu.roll(mine, (-shift) % LANE, 1)
            cube = total + 0.044715 * total * total * total
            gelu = 0.5 * total * (1.0 + jnp.tanh(math.sqrt(2.0 / math.pi) * cube))
            states[first_block + r] = own[r, :, lon * LANE : (lon + 1) * LANE] + gelu

    def fwd_copy(s, to, source):
        return pltpu.make_async_remote_copy(
            src_ref=states.at[n_ens * s + to] if s < slots else states.at[BLOCKS - 1],
            dst_ref=recv.at[s, source],
            send_sem=fwd_send.at[s, to],
            recv_sem=fwd_recv.at[s, source],
            device_id=place(to, lat),
            device_id_type=MESH,
        )

    def send_slot(s):
        for k in range(1, n_ens):
            fwd_copy(s, ens_peer(k), me).start()
        recv[s, me] = states[n_ens * s + me]

    for chunk in (0, 1):
        wait_halo(far, chunk)
        add_side(far, chunk)
    finish(1, 0)
    finish(2, 5)
    send_slot(0)
    wait_halo(far, 2)
    add_side(far, 2)
    finish(3, 10)
    for s in range(1, slots):
        if n_ens * (s + 1) <= 15:
            send_slot(s)
    finish(4, 15)
    finish(0, 20)
    for s in range(1, slots):
        if n_ens * (s + 1) > 15:
            send_slot(s)

    @pl.when(me != extra)
    def _():
        fwd_copy(slots, extra, me).start()

    pairs = [(a, b) for a in range(n_ens) for b in range(a + 1, n_ens)]

    def back_copy(s, b, r, lon, to):
        return pltpu.make_async_remote_copy(
            src_ref=grads.at[s, to],
            dst_ref=out_ref.at[r, 0, :, pl.ds(pl.multiple_of(lon * LANE, LANE), LANE)],
            send_sem=back_send.at[s, to],
            recv_sem=back_recv.at[b],
            device_id=place(to, lat),
            device_id_type=MESH,
        )

    def self_copy(s, r, lon):
        return pltpu.make_async_copy(
            grads.at[s, me],
            out_ref.at[r, 0, :, pl.ds(pl.multiple_of(lon * LANE, LANE), LANE)],
            self_sem.at[s],
        )

    def measure(s, b):
        r, lon = block_place(b)
        for k in range(1, n_ens):
            fwd_copy(s, me, ens_peer(k)).wait_recv()
        area = area_ref[first + r]

        def square(v, sums):
            rows = pl.ds(pl.multiple_of(v * 8, 8), 8)
            x = [recv[s, m, rows, :] for m in range(n_ens)]
            goal = target[s, rows, :]
            gaps = [xm - goal for xm in x] + [x[a] - x[c] for a, c in pairs]
            return tuple(total + gap * gap for total, gap in zip(sums, gaps))

        zero = jnp.zeros((8, LANE), F32)
        sums = lax.fori_loop(0, C // 8, square, (zero,) * (n_ens + len(pairs)))
        skill_sum = jnp.zeros((1, LANE), F32)
        pair_sum = jnp.zeros((1, LANE), F32)
        for at, total in enumerate(sums):
            mean = jnp.sum(total, axis=0, keepdims=True) * (1.0 / C) + 1.0
            inverse = lax.rsqrt(mean)
            if at < n_ens:
                skill_sum = skill_sum + mean * inverse
                pulls[s, at] = jnp.broadcast_to(inverse * area, (8, LANE))
            else:
                pair_sum = pair_sum + mean * inverse
                pulls[s, at] = jnp.broadcast_to(inverse * (area * (1.0 / n_ens)), (8, LANE))
        cell = skill_sum * (1.0 / n_ens) - (2.0 * pair_sum + n_ens) * (1.0 / (2 * n_ens * n_ens))
        return jnp.broadcast_to(area * cell, (8, LANE))

    def give_back(s, b):
        r, lon = block_place(b)

        @pl.loop(0, C // 8)
        def _(v):
            rows = pl.ds(pl.multiple_of(v * 8, 8), 8)
            x = [recv[s, m, rows, :] for m in range(n_ens)]
            goal = target[s, rows, :]
            g = [(x[m] - goal) * pulls[s, m] for m in range(n_ens)]
            for at, (a, c) in enumerate(pairs):
                pull = (x[a] - x[c]) * pulls[s, n_ens + at]
                g[a] = g[a] - pull
                g[c] = g[c] + pull
            for m in range(n_ens):
                grads[s, m, rows, :] = g[m]

        for k in range(1, n_ens):
            back_copy(s, b, r, lon, ens_peer(k)).start()
        self_copy(s, r, lon).start()

    class Level:
        def __init__(self, buf, send, got, count, mine, peer):
            self.buf, self.send, self.got = buf, send, got
            self.count, self.mine, self.peer = count, mine, peer

        def copy(self, k, slot):
            return pltpu.make_async_remote_copy(
                src_ref=self.buf.at[self.mine],
                dst_ref=self.buf.at[slot],
                send_sem=self.send.at[k],
                recv_sem=self.got.at[slot],
                device_id=self.peer(k),
                device_id_type=MESH,
            )

        def start(self):
            for k in range(1, self.count):
                self.copy(k, self.mine).start()

        def total(self):
            for k in range(1, self.count):
                self.copy(k, lax.rem(self.mine + k, self.count)).wait_recv()
            total = self.buf[0]
            for k in range(1, self.count):
                total = total + self.buf[k]
            return total

        def sent(self):
            for k in range(1, self.count):
                self.copy(k, self.mine).wait_send()

    level1 = Level(lossbuf1, l1_send, l1_recv, n_ens, me, lambda k: place(ens_peer(k), lat))
    level2 = Level(lossbuf2, l2_send, l2_recv, group, inner, lambda k: place(me, inner_peer(k)))
    level3 = Level(lossbuf3, l3_send, l3_recv, tall, outer, lambda k: place(me, outer_peer(k)))

    part = measure(0, me)
    give_back(0, me)
    for s in range(1, slots):
        part = part + measure(s, n_ens * s + me)
    lossbuf1[me] = part

    @pl.when(me == extra)
    def _():
        recv[slots, me] = states[BLOCKS - 1]
        lossbuf1[me] += measure(slots, BLOCKS - 1)

    level1.start()
    give_back(1, n_ens + me)
    lossbuf2[inner] = level1.total()
    level2.start()
    for s in range(2, slots):
        give_back(s, n_ens * s + me)

    @pl.when(me == extra)
    def _():
        give_back(slots, BLOCKS - 1)

    lossbuf3[outer] = level2.total()
    level3.start()
    total = level3.total()
    loss_ref[0] = jnp.sum(total[0:1, :]) * (1.0 / (n_lat * ROWS * NLON))

    def wait_back(b, owner):
        @pl.when(me != owner)
        def _():
            r, lon = block_place(b)
            back_copy(0, b, r, lon, me).wait_recv()

    for s in range(slots):
        b = n_ens * s + me
        self_copy(s, *block_place(b)).wait()
        for k in range(1, n_ens):
            to = ens_peer(k)
            c = n_ens * s + to
            back_copy(s, c, *block_place(c), me).wait_recv()
            back_copy(s, b, *block_place(b), to).wait_send()
            fwd_copy(s, to, me).wait_send()
    last = BLOCKS - 1

    @pl.when(me == extra)
    def _():
        self_copy(slots, *block_place(last)).wait()
        for k in range(1, n_ens):
            back_copy(slots, last, *block_place(last), ens_peer(k)).wait_send()

    @pl.when(me != extra)
    def _():
        back_copy(slots, last, *block_place(last), me).wait_recv()
        fwd_copy(slots, extra, me).wait_send()

    for level in (level1, level2, level3):
        level.sent()

    def sent(side, there):
        @pl.when(there)
        def _():
            for chunk in range(len(CHUNKS)):
                halo_copy(side, chunk).wait_send()

    sent(0, has_up)
    sent(1, has_down)


def area_weights(total_rows):
    latitude = (np.arange(total_rows, dtype=np.float64) + 0.5) * (math.pi / total_rows) - 0.5 * math.pi
    cosine = np.cos(latitude)
    return (cosine / np.mean(cosine)).astype(np.float32)


def per_device(n_ens, n_lat, members, truth, target_time, row_taps, filters, mixing):
    taps = jnp.transpose(row_taps, (1, 0, 2))
    spread = jnp.transpose(filters, (1, 2, 4, 0, 3)).reshape(ROWS * TAPS * LW, 1, K)
    mix = jnp.transpose(mixing[0], (1, 0, 2))
    area = jnp.asarray(area_weights(n_lat * ROWS))
    slots = BLOCKS // n_ens
    group = min(8, n_lat)
    tall = n_lat // group
    vmem = pltpu.VMEM
    dma = pltpu.SemaphoreType.DMA
    smem = pltpu.SMEM
    smem_spec = pl.BlockSpec(memory_space=pltpu.SMEM)
    any_spec = pl.BlockSpec(memory_space=pl.ANY)
    hbm_spec = pl.BlockSpec(memory_space=pltpu.HBM)
    return pl.pallas_call(
        functools.partial(kernel, n_ens, n_lat),
        out_shape=(
            pltpu.VMEM((ROWS, 1, C, NLON), F32),
            jax.ShapeDtypeStruct((1,), F32),
        ),
        in_specs=[hbm_spec] * 7,
        out_specs=(any_spec, smem_spec),
        scratch_shapes=[
            smem((ROWS, 1, TAPS), jnp.int32),
            smem((ROWS,), jnp.int32),
            smem((n_lat * ROWS,), F32),
            vmem((ROWS * TAPS * LW, 1, K), F32),
            vmem((K, C, C), F32),
            vmem((ROWS, C, NLON), F32),
            vmem((2, REACH, C, NLON), F32),
            vmem((OWN_PAD, NLON), BF16),
            vmem((OWN_PAD, NLON), BF16),
            vmem((SIDE, NLON), BF16),
            vmem((SIDE, NLON), BF16),
            vmem((LANE, LANE), F32),
            vmem((K, C, LANE), F32),
            vmem((ROWS * LW, KP, OWN_PAD), F32),
            vmem((2, ROWS * LW, KP, SIDE), F32),
            vmem((ROWS * BAND, OWN_PAD), BF16),
            vmem((ROWS * BAND, OWN_PAD), BF16),
            vmem((REACH * BAND, SIDE), BF16),
            vmem((REACH * BAND, SIDE), BF16),
            vmem((ROWS * BAND, NLON), F32),
            vmem((BLOCKS, C, LANE), F32),
            vmem((slots + 1, n_ens, C, LANE), F32),
            vmem((slots + 1, n_ens, C, LANE), F32),
            vmem((slots + 1, 4, C, LANE), F32),
            vmem((slots + 1, C, LANE), F32),
            vmem((slots + 1, n_ens * (n_ens + 1) // 2, 8, LANE), F32),
            vmem((n_ens, 8, LANE), F32),
            vmem((group, 8, LANE), F32),
            vmem((tall, 8, LANE), F32),
            dma((5,)),
            dma,
            dma((slots + 1,)),
            dma((2, len(CHUNKS))),
            dma((2, len(CHUNKS))),
            dma((slots + 1, n_ens)),
            dma((slots + 1, n_ens)),
            dma((slots + 1, n_ens)),
            dma((BLOCKS,)),
            dma((slots + 1,)),
            dma((n_ens,)),
            dma((n_ens,)),
            dma((group,)),
            dma((group,)),
            dma((tall,)),
            dma((tall,)),
        ],
        compiler_params=pltpu.CompilerParams(
            collective_id=0, has_side_effects=True, vmem_limit_bytes=54 * 2**20
        ),
        cost_estimate=pl.CostEstimate(flops=5_000_000_000, bytes_accessed=4_000_000, transcendentals=400_000),
    )(taps, target_time, area, spread, mix, members, truth)


def solution(mesh):
    placed = (
        P("lat", "ens", None, None),
        P(None, "lat", None, None),
        P("lat"),
        P(None, "lat", None),
        P(None, "lat", None, None, None),
        P(),
    )
    return jax.shard_map(
        functools.partial(per_device, mesh.shape["ens"], mesh.shape["lat"]),
        mesh=mesh,
        in_specs=placed,
        out_specs=(P("lat", "ens", None, None), P()),
        check_vma=False,
    )
```

```python
import functools
import math

import jax
import jax.numpy as jnp
import numpy as np
from jax import lax
from jax.experimental import pallas as pl
from jax.experimental.pallas import tpu as pltpu
from jax.sharding import PartitionSpec as P

C = 64
NLON = 640
K = 9
KP = 16
TAPS = 5
LW = 5
REACH = 4
ROWS = 5
LANE = 128
NB = NLON // LANE
BLOCKS = ROWS * NB
SIDE = REACH * C
OWN = ROWS * C
OWN_PAD = 384
BAND = LW * C
MESH = pl.DeviceIdType.MESH
CHUNKS = ((0, 256), (256, 256), (512, 128))
F32 = jnp.float32
BF16 = jnp.bfloat16


def split(x):
    hi = x.astype(BF16)
    return hi, (x - hi.astype(F32)).astype(BF16)


def dot(w, x):
    return jnp.dot(w, x, preferred_element_type=F32)


def place_of(core, b):
    order = b // NB
    return jnp.where(core == 0, ROWS - 1 - order, order), lax.rem(b, NB)


def kernel(
    n_ens,
    n_lat,
    taps_hbm,
    time_hbm,
    area_hbm,
    filt_hbm,
    mix_hbm,
    members_ref,
    truth_ref,
    out_ref,
    loss_ref,
    taps_ref,
    time_ref,
    area_ref,
    filt_ref,
    mix_ref,
    own,
    halo,
    own_x,
    near_x,
    far_x,
    rows_in,
    mdup,
    a_own,
    a_side,
    w_own,
    w_side,
    acc,
    states,
    recv,
    grads,
    cand,
    target,
    pulls,
    lossbuf1,
    lossbuf2,
    lossbuf3,
    small_sem,
    own_sem,
    cand_sem,
    halo_send,
    halo_recv,
    fwd_send,
    fwd_recv,
    back_send,
    back_recv,
    self_sem,
    l1_send,
    l1_recv,
    l2_send,
    l2_recv,
    l3_send,
    l3_recv,
):
    me = lax.axis_index("ens")
    lat = lax.axis_index("lat")
    group = min(8, n_lat)
    tall = n_lat // group
    first = lat * ROWS
    core = lax.rem(lat, 2)
    near = 1 - core
    far = core
    slots = BLOCKS // n_ens
    extra = lax.rem(core * (n_ens // 2) + lax.rem(lat // 2, n_ens // 2), n_ens)
    inner = lax.rem(lat, group)
    outer = lat // group
    has_up = lat < n_lat - 1
    has_down = lat > 0

    half = n_ens // 2
    block_place = functools.partial(place_of, core)

    def block_of(s, owner):
        return n_ens * s + lax.rem(owner, half) * 2 + owner // half

    def place(ens_at, lat_at):
        return {"ens": ens_at, "lat": lat_at}

    def ens_peer(k):
        return lax.rem(me + k, n_ens)

    def inner_peer(k):
        return outer * group + lax.rem(inner + k, group)

    def outer_peer(k):
        return lax.rem(outer + k, tall) * group + inner

    barrier = pltpu.get_barrier_semaphore()
    for k in range(1, n_ens):
        pl.semaphore_signal(barrier, inc=1, device_id=place(ens_peer(k), lat), device_id_type=MESH)
    for k in range(1, group):
        pl.semaphore_signal(barrier, inc=1, device_id=place(me, inner_peer(k)), device_id_type=MESH)
    for k in range(1, tall):
        pl.semaphore_signal(barrier, inc=1, device_id=place(me, outer_peer(k)), device_id_type=MESH)
    over_up = has_up & (inner == group - 1)
    over_down = has_down & (inner == 0)

    @pl.when(over_up)
    def _():
        pl.semaphore_signal(barrier, inc=1, device_id=place(me, lat + 1), device_id_type=MESH)

    @pl.when(over_down)
    def _():
        pl.semaphore_signal(barrier, inc=1, device_id=place(me, lat - 1), device_id_type=MESH)

    smalls = [
        pltpu.make_async_copy(source, kept, small_sem.at[at])
        for at, (source, kept) in enumerate(
            (
                (mix_hbm, mix_ref),
                (filt_hbm, filt_ref),
                (taps_hbm, taps_ref),
                (time_hbm, time_ref),
                (area_hbm, area_ref),
            )
        )
    ]
    for small in smalls:
        small.start()
    own_copy = pltpu.make_async_copy(members_ref.at[:, 0], own, own_sem)
    own_copy.start()

    def cand_copy(s):
        r, lon = block_place(block_of(s, me))
        return pltpu.make_async_copy(
            truth_ref.at[:, r, :, pl.ds(pl.multiple_of(lon * LANE, LANE), LANE)], cand.at[s], cand_sem.at[s]
        )

    def extra_copy():
        r, _ = block_place(BLOCKS - 1)
        return pltpu.make_async_copy(
            truth_ref.at[:, r, :, pl.ds((NB - 1) * LANE, LANE)], cand.at[slots], cand_sem.at[slots]
        )

    for s in range(slots):
        cand_copy(s).start()

    @pl.when(me == extra)
    def _():
        extra_copy().start()

    greeted = n_ens - 1 + group - 1 + tall - 1
    pl.semaphore_wait(barrier, greeted + over_up.astype(jnp.int32) + over_down.astype(jnp.int32))

    def halo_copy(side, step):
        row = REACH - 1 - step if side == 0 else step
        to = lat + 1 if side == 0 else lat - 1
        return pltpu.make_async_remote_copy(
            src_ref=members_ref.at[row + 1 - side, 0],
            dst_ref=halo.at[side, row],
            send_sem=halo_send.at[side, step],
            recv_sem=halo_recv.at[side, step],
            device_id=place(me, to),
            device_id_type=MESH,
        )

    def send_side(side):
        for step in range(REACH):
            halo_copy(side, step).start()

    @pl.when((core == 1) & has_up)
    def _():
        send_side(0)

    @pl.when((core == 0) & has_down)
    def _():
        send_side(1)

    @pl.when((core == 0) & has_up)
    def _():
        send_side(0)

    @pl.when((core == 1) & has_down)
    def _():
        send_side(1)

    for small in smalls:
        small.wait()

    for k in range(K):
        mdup[k] = jnp.concatenate([mix_ref[k], mix_ref[k]], axis=1)

    def row_of(width, low, high):
        lane = lax.broadcasted_iota(jnp.int32, (1, width), 1)
        q = low + lane // C
        return jnp.where(q < high, q, -1)

    q_own = jnp.minimum(row_of(OWN_PAD, REACH, REACH + ROWS + 1), REACH + ROWS - 1)
    q_sides = (row_of(SIDE, 0, REACH), row_of(SIDE, REACH + ROWS, ROWS + 2 * REACH))

    for i in range(ROWS * TAPS * LW):
        rows_in[i : i + 1, :K] = filt_ref[i]
    turned = jnp.transpose(rows_in[...])[:KP]

    for r in range(ROWS):
        hits = [
            [(q == taps_ref[r, 0, t] - first + REACH).astype(F32) for t in range(TAPS)] for q in (q_own, *q_sides)
        ]
        for d in range(LW):
            columns = [(r * TAPS + t) * LW + d for t in range(TAPS)]
            columns = [jnp.broadcast_to(turned[:, at : at + 1], (KP, LANE)) for at in columns]
            for ref, hit in zip((a_own, a_side.at[0], a_side.at[1]), hits):
                for at in range(0, ref.shape[2], LANE):
                    terms = [columns[t] * hit[t][:, at : at + LANE] for t in range(TAPS)]
                    ref[r * LW + d, :, at : at + LANE] = functools.reduce(jnp.add, terms)

    def weights(rd, a_at, width):
        for at in range(0, width, LANE):
            total = None
            for k in range(K):
                term = a_at[rd, k : k + 1, at : at + LANE] * mdup[k]
                total = term if total is None else total + term
            yield at, split(total)

    in_low = lax.broadcasted_iota(jnp.int32, (C, LANE), 1) < C

    @pl.loop(0, ROWS * LW)
    def _(rd):
        rows = pl.ds(pl.multiple_of(rd * C, C), C)
        for at, (hi, lo) in weights(rd, a_own, OWN_PAD):
            if at < SIDE:
                w_own[rows, at : at + LANE] = hi
                w_own[rows, SIDE + at : SIDE + at + LANE] = hi
                w_own[rows, 2 * SIDE + at : 2 * SIDE + at + LANE] = lo
            else:
                w_own[rows, 3 * SIDE : 3 * SIDE + LANE] = hi
                w_own[rows, 3 * SIDE + LANE :] = jnp.where(in_low, lo, jnp.zeros_like(lo))

    own_copy.wait()
    hi, lo = split(own[:REACH].reshape(SIDE, NLON))
    own_x[:SIDE] = hi
    own_x[SIDE : 2 * SIDE] = lo
    own_x[2 * SIDE : 3 * SIDE] = hi
    hi, lo = split(own[REACH])
    own_x[3 * SIDE : 3 * SIDE + C] = hi
    own_x[3 * SIDE + C : 3 * SIDE + 2 * C] = lo
    own_x[3 * SIDE + 2 * C : 3 * SIDE + 3 * C] = hi
    own_x[3 * SIDE + 3 * C :] = jnp.zeros((C, NLON), BF16)

    @pl.loop(0, ROWS)
    def _(r):
        rows = pl.ds(pl.multiple_of(r * BAND, BAND), BAND)
        for start, width in CHUNKS:
            lons = pl.ds(start, width)
            acc[rows, lons] = dot(w_own[rows, :], own_x[:, lons])

    def side_weights(side):
        a_at = a_side.at[side]

        @pl.loop(0, REACH * LW)
        def _(i):
            rows = pl.ds(pl.multiple_of(i * C, C), C)
            for at, (hi, lo) in weights(i + side * LW, a_at, SIDE):
                w_side[rows, at : at + LANE] = hi
                w_side[rows, SIDE + at : SIDE + at + LANE] = hi
                w_side[rows, 2 * SIDE + at : 2 * SIDE + at + LANE] = lo

    def add_row(side, i, x_ref):
        rows = pl.ds(pl.multiple_of(i * BAND, BAND), BAND)
        acc_rows = pl.ds(pl.multiple_of((i + side) * BAND, BAND), BAND)
        for start, width in CHUNKS:
            lons = pl.ds(start, width)
            acc[acc_rows, lons] += dot(w_side[rows, :], x_ref[:, lons])

    side_weights(near)
    far_x[...] = jnp.zeros_like(far_x)
    for side in range(2):

        @pl.when(near == side)
        def _():
            for step in range(REACH):
                halo_copy(side, step).wait_recv()

    hi, lo = split(halo[near].reshape(SIDE, NLON))
    near_x[:SIDE] = hi
    near_x[SIDE : 2 * SIDE] = lo
    near_x[2 * SIDE :] = hi

    @pl.loop(0, REACH)
    def _(i):
        add_row(near, i, near_x)

    side_weights(far)

    def pick_target(s, r):
        time = time_ref[r]
        picked = cand[s, 0]
        for t in range(1, 4):
            picked = jnp.where(time == t, cand[s, t], picked)
        target[s] = picked

    for s in range(slots):
        cand_copy(s).wait()
        pick_target(s, block_place(block_of(s, me))[0])

    @pl.when(me == extra)
    def _():
        extra_copy().wait()
        pick_target(slots, block_place(BLOCKS - 1)[0])

    lane = lax.broadcasted_iota(jnp.int32, (C, LANE), 1)

    def finish(order):
        r, _ = block_place(order * NB)

        def part(d, at):
            rows = pl.ds(pl.multiple_of(r * BAND + d * C, C), C)
            at = at % NB
            return acc[rows, at * LANE : (at + 1) * LANE]

        for lon in range(NB):
            total = part(2, lon)
            for d in (0, 1, 3, 4):
                shift = d - LW // 2
                if shift > 0:
                    mine = jnp.where(lane < shift, part(d, lon + 1), part(d, lon))
                else:
                    mine = jnp.where(lane >= LANE + shift, part(d, lon - 1), part(d, lon))
                total = total + pltpu.roll(mine, (-shift) % LANE, 1)
            cube = total + 0.044715 * total * total * total
            gelu = 0.5 * total * (1.0 + jnp.tanh(math.sqrt(2.0 / math.pi) * cube))
            states[order * NB + lon] = own[r, :, lon * LANE : (lon + 1) * LANE] + gelu

    def fwd_copy(s, to, source):
        return pltpu.make_async_remote_copy(
            src_ref=states.at[block_of(s, to)] if s < slots else states.at[BLOCKS - 1],
            dst_ref=recv.at[s, source],
            send_sem=fwd_send.at[s, to],
            recv_sem=fwd_recv.at[s, source],
            device_id=place(to, lat),
            device_id_type=MESH,
        )

    def send_row(order):
        for b in range(order * NB, (order + 1) * NB):
            s, j = divmod(b, n_ens)
            to = j % 2 * half + j // 2 if s < slots else extra

            @pl.when(me != to)
            def _():
                fwd_copy(s, to, me).start()

            @pl.when(me == to)
            def _():
                recv[s, me] = states[b]

    finish(0)
    send_row(0)
    for step in range(REACH):
        for side, there in ((0, has_down), (1, has_up)):

            @pl.when((far == side) & there)
            def _():
                halo_copy(side, step).wait_recv()
                row = REACH - 1 - step if side == 0 else step
                hi, lo = split(halo[side, row])
                far_x[row * C : (row + 1) * C] = hi
                far_x[SIDE + row * C : SIDE + (row + 1) * C] = lo
                far_x[2 * SIDE + row * C : 2 * SIDE + (row + 1) * C] = hi

        add_row(far, jnp.where(far == 0, REACH - 1 - step, step), far_x)
        finish(step + 1)
        send_row(step + 1)

    pairs = [(a, b) for a in range(n_ens) for b in range(a + 1, n_ens)]

    def back_copy(s, b, r, lon, to):
        return pltpu.make_async_remote_copy(
            src_ref=grads.at[s, to],
            dst_ref=out_ref.at[r, 0, :, pl.ds(pl.multiple_of(lon * LANE, LANE), LANE)],
            send_sem=back_send.at[s, to],
            recv_sem=back_recv.at[b],
            device_id=place(to, lat),
            device_id_type=MESH,
        )

    def self_copy(s, r, lon):
        return pltpu.make_async_copy(
            grads.at[s, me],
            out_ref.at[r, 0, :, pl.ds(pl.multiple_of(lon * LANE, LANE), LANE)],
            self_sem.at[s],
        )

    def measure(s, b):
        r, lon = block_place(b)
        for k in range(1, n_ens):
            fwd_copy(s, me, ens_peer(k)).wait_recv()
        area = area_ref[first + r]

        def square(v, sums):
            rows = pl.ds(pl.multiple_of(v * 8, 8), 8)
            x = [recv[s, m, rows, :] for m in range(n_ens)]
            goal = target[s, rows, :]
            gaps = [xm - goal for xm in x] + [x[a] - x[c] for a, c in pairs]
            return tuple(total + gap * gap for total, gap in zip(sums, gaps))

        zero = jnp.zeros((8, LANE), F32)
        sums = lax.fori_loop(0, C // 8, square, (zero,) * (n_ens + len(pairs)))
        skill_sum = jnp.zeros((1, LANE), F32)
        pair_sum = jnp.zeros((1, LANE), F32)
        for at, total in enumerate(sums):
            mean = jnp.sum(total, axis=0, keepdims=True) * (1.0 / C) + 1.0
            inverse = lax.rsqrt(mean)
            if at < n_ens:
                skill_sum = skill_sum + mean * inverse
                pulls[s, at] = jnp.broadcast_to(inverse * area, (8, LANE))
            else:
                pair_sum = pair_sum + mean * inverse
                pulls[s, at] = jnp.broadcast_to(inverse * (area * (1.0 / n_ens)), (8, LANE))
        cell = skill_sum * (1.0 / n_ens) - (2.0 * pair_sum + n_ens) * (1.0 / (2 * n_ens * n_ens))
        return jnp.broadcast_to(area * cell, (8, LANE))

    def give_back(s, b):
        r, lon = block_place(b)

        @pl.loop(0, C // 8)
        def _(v):
            rows = pl.ds(pl.multiple_of(v * 8, 8), 8)
            x = [recv[s, m, rows, :] for m in range(n_ens)]
            goal = target[s, rows, :]
            g = [(x[m] - goal) * pulls[s, m] for m in range(n_ens)]
            for at, (a, c) in enumerate(pairs):
                pull = (x[a] - x[c]) * pulls[s, n_ens + at]
                g[a] = g[a] - pull
                g[c] = g[c] + pull
            for m in range(n_ens):
                grads[s, m, rows, :] = g[m]

        for k in range(1, n_ens):
            back_copy(s, b, r, lon, ens_peer(k)).start()
        self_copy(s, r, lon).start()

    class Level:
        def __init__(self, buf, send, got, count, mine, peer):
            self.buf, self.send, self.got = buf, send, got
            self.count, self.mine, self.peer = count, mine, peer

        def copy(self, k, slot):
            return pltpu.make_async_remote_copy(
                src_ref=self.buf.at[self.mine],
                dst_ref=self.buf.at[slot],
                send_sem=self.send.at[k],
                recv_sem=self.got.at[slot],
                device_id=self.peer(k),
                device_id_type=MESH,
            )

        def start(self):
            for k in range(1, self.count):
                self.copy(k, self.mine).start()

        def total(self):
            for k in range(1, self.count):
                self.copy(k, lax.rem(self.mine + k, self.count)).wait_recv()
            total = self.buf[0]
            for k in range(1, self.count):
                total = total + self.buf[k]
            return total

        def sent(self):
            for k in range(1, self.count):
                self.copy(k, self.mine).wait_send()

    level1 = Level(lossbuf1, l1_send, l1_recv, n_ens, me, lambda k: place(ens_peer(k), lat))
    level2 = Level(lossbuf2, l2_send, l2_recv, group, inner, lambda k: place(me, inner_peer(k)))
    level3 = Level(lossbuf3, l3_send, l3_recv, tall, outer, lambda k: place(me, outer_peer(k)))

    part = measure(0, block_of(0, me))
    give_back(0, block_of(0, me))
    part = part + measure(1, block_of(1, me))
    part = part + measure(2, block_of(2, me))
    lossbuf2[inner] = part

    @pl.when(me == extra)
    def _():
        lossbuf2[inner] += measure(slots, BLOCKS - 1)

    level2.start()
    give_back(1, block_of(1, me))
    lossbuf3[outer] = level2.total()
    level3.start()
    give_back(2, block_of(2, me))

    @pl.when(me == extra)
    def _():
        give_back(slots, BLOCKS - 1)

    lossbuf1[me] = level3.total()
    level1.start()
    total = level1.total()
    loss_ref[0] = jnp.sum(total[0:1, :]) * (1.0 / (n_lat * ROWS * NLON))

    for s in range(slots):
        b = block_of(s, me)
        self_copy(s, *block_place(b)).wait()
        for k in range(1, n_ens):
            to = ens_peer(k)
            c = block_of(s, to)
            back_copy(s, c, *block_place(c), me).wait_recv()
            back_copy(s, b, *block_place(b), to).wait_send()
            fwd_copy(s, to, me).wait_send()
    last = BLOCKS - 1

    @pl.when(me == extra)
    def _():
        self_copy(slots, *block_place(last)).wait()
        for k in range(1, n_ens):
            back_copy(slots, last, *block_place(last), ens_peer(k)).wait_send()

    @pl.when(me != extra)
    def _():
        back_copy(slots, last, *block_place(last), me).wait_recv()
        fwd_copy(slots, extra, me).wait_send()

    for level in (level1, level2, level3):
        level.sent()

    def sent(side, there):
        @pl.when(there)
        def _():
            for step in range(REACH):
                halo_copy(side, step).wait_send()

    sent(0, has_up)
    sent(1, has_down)


def area_weights(total_rows):
    latitude = (np.arange(total_rows, dtype=np.float64) + 0.5) * (math.pi / total_rows) - 0.5 * math.pi
    cosine = np.cos(latitude)
    return (cosine / np.mean(cosine)).astype(np.float32)


def per_device(n_ens, n_lat, members, truth, target_time, row_taps, filters, mixing):
    taps = jnp.transpose(row_taps, (1, 0, 2))
    spread = jnp.transpose(filters, (1, 2, 4, 0, 3)).reshape(ROWS * TAPS * LW, 1, K)
    mix = jnp.transpose(mixing[0], (1, 0, 2))
    area = jnp.asarray(area_weights(n_lat * ROWS))
    slots = BLOCKS // n_ens
    group = min(8, n_lat)
    tall = n_lat // group
    vmem = pltpu.VMEM
    dma = pltpu.SemaphoreType.DMA
    smem = pltpu.SMEM
    smem_spec = pl.BlockSpec(memory_space=pltpu.SMEM)
    any_spec = pl.BlockSpec(memory_space=pl.ANY)
    hbm_spec = pl.BlockSpec(memory_space=pltpu.HBM)
    return pl.pallas_call(
        functools.partial(kernel, n_ens, n_lat),
        out_shape=(
            pltpu.VMEM((ROWS, 1, C, NLON), F32),
            jax.ShapeDtypeStruct((1,), F32),
        ),
        in_specs=[hbm_spec] * 7,
        out_specs=(any_spec, smem_spec),
        scratch_shapes=[
            smem((ROWS, 1, TAPS), jnp.int32),
            smem((ROWS,), jnp.int32),
            smem((n_lat * ROWS,), F32),
            vmem((ROWS * TAPS * LW, 1, K), F32),
            vmem((K, C, C), F32),
            vmem((ROWS, C, NLON), F32),
            vmem((2, REACH, C, NLON), F32),
            vmem((4 * SIDE, NLON), BF16),
            vmem((3 * SIDE, NLON), BF16),
            vmem((3 * SIDE, NLON), BF16),
            vmem((LANE, LANE), F32),
            vmem((K, C, LANE), F32),
            vmem((ROWS * LW, KP, OWN_PAD), F32),
            vmem((2, ROWS * LW, KP, SIDE), F32),
            vmem((ROWS * BAND, 4 * SIDE), BF16),
            vmem((REACH * BAND, 3 * SIDE), BF16),
            vmem((ROWS * BAND, NLON), F32),
            vmem((BLOCKS, C, LANE), F32),
            vmem((slots + 1, n_ens, C, LANE), F32),
            vmem((slots + 1, n_ens, C, LANE), F32),
            vmem((slots + 1, 4, C, LANE), F32),
            vmem((slots + 1, C, LANE), F32),
            vmem((slots + 1, n_ens * (n_ens + 1) // 2, 8, LANE), F32),
            vmem((n_ens, 8, LANE), F32),
            vmem((group, 8, LANE), F32),
            vmem((tall, 8, LANE), F32),
            dma((5,)),
            dma,
            dma((slots + 1,)),
            dma((2, REACH)),
            dma((2, REACH)),
            dma((slots + 1, n_ens)),
            dma((slots + 1, n_ens)),
            dma((slots + 1, n_ens)),
            dma((BLOCKS,)),
            dma((slots + 1,)),
            dma((n_ens,)),
            dma((n_ens,)),
            dma((group,)),
            dma((group,)),
            dma((tall,)),
            dma((tall,)),
        ],
        compiler_params=pltpu.CompilerParams(
            collective_id=0, has_side_effects=True, vmem_limit_bytes=54 * 2**20
        ),
        cost_estimate=pl.CostEstimate(flops=5_000_000_000, bytes_accessed=4_000_000, transcendentals=400_000),
    )(taps, target_time, area, spread, mix, members, truth)


def solution(mesh):
    placed = (
        P("lat", "ens", None, None),
        P(None, "lat", None, None),
        P("lat"),
        P(None, "lat", None),
        P(None, "lat", None, None, None),
        P(),
    )
    return jax.shard_map(
        functools.partial(per_device, mesh.shape["ens"], mesh.shape["lat"]),
        mesh=mesh,
        in_specs=placed,
        out_specs=(P("lat", "ens", None, None), P()),
        check_vma=False,
    )
```

```python
import functools
import math

import jax
import jax.numpy as jnp
import numpy as np
from jax import lax
from jax.experimental import pallas as pl
from jax.experimental.pallas import tpu as pltpu
from jax.sharding import PartitionSpec as P

C = 64
NLON = 640
K = 9
KP = 16
TAPS = 5
LW = 5
REACH = 4
ROWS = 5
LANE = 128
NB = NLON // LANE
BLOCKS = ROWS * NB
SIDE = REACH * C
OWN = ROWS * C
OWN_PAD = 384
BAND = LW * C
MESH = pl.DeviceIdType.MESH
CHUNKS = ((0, 256), (256, 256), (512, 128))
F32 = jnp.float32
BF16 = jnp.bfloat16


def split(x):
    hi = x.astype(BF16)
    return hi, (x - hi.astype(F32)).astype(BF16)


def dot(w, x):
    return jnp.dot(w, x, preferred_element_type=F32)


def far_first(count):
    return sorted(range(1, count), key=lambda k: -min(k, count - k))


def place_of(core, b):
    order = b // NB
    return jnp.where(core == 0, ROWS - 1 - order, order), lax.rem(b, NB)


def kernel(
    n_ens,
    n_lat,
    taps_hbm,
    time_hbm,
    area_hbm,
    filt_hbm,
    mix_hbm,
    members_ref,
    truth_ref,
    out_ref,
    loss_ref,
    taps_ref,
    time_ref,
    area_ref,
    filt_ref,
    mix_ref,
    own,
    halo,
    own_x,
    near_x,
    far_x,
    rows_in,
    mdup,
    a_own,
    a_side,
    w_own,
    w_side,
    acc,
    states,
    recv,
    grads,
    cand,
    target,
    pulls,
    lossbuf1,
    lossbuf2,
    lossbuf3,
    small_sem,
    own_sem,
    cand_sem,
    halo_send,
    halo_recv,
    fwd_send,
    fwd_recv,
    back_send,
    back_recv,
    self_sem,
    l1_send,
    l1_recv,
    l2_send,
    l2_recv,
    l3_send,
    l3_recv,
):
    me = lax.axis_index("ens")
    lat = lax.axis_index("lat")
    group = min(8, n_lat)
    tall = n_lat // group
    first = lat * ROWS
    core = lax.rem(lat, 2)
    near = 1 - core
    far = core
    slots = BLOCKS // n_ens
    extra = lax.rem(core * (n_ens // 2) + lax.rem(lat // 2, n_ens // 2), n_ens)
    inner = lax.rem(lat, group)
    outer = lat // group
    has_up = lat < n_lat - 1
    has_down = lat > 0

    half = n_ens // 2
    block_place = functools.partial(place_of, core)

    def block_of(s, owner):
        return n_ens * s + lax.rem(owner, half) * 2 + owner // half

    def place(ens_at, lat_at):
        return {"ens": ens_at, "lat": lat_at}

    def ens_peer(k):
        return lax.rem(me + k, n_ens)

    def inner_peer(k):
        return outer * group + lax.rem(inner + k, group)

    def outer_peer(k):
        return lax.rem(outer + k, tall) * group + inner

    barrier = pltpu.get_barrier_semaphore()
    for k in far_first(group):
        pl.semaphore_signal(barrier, inc=1, device_id=place(me, inner_peer(k)), device_id_type=MESH)
    for k in far_first(n_ens):
        pl.semaphore_signal(barrier, inc=1, device_id=place(ens_peer(k), lat), device_id_type=MESH)
    for k in range(1, tall):
        pl.semaphore_signal(barrier, inc=1, device_id=place(me, outer_peer(k)), device_id_type=MESH)
    over_up = has_up & (inner == group - 1)
    over_down = has_down & (inner == 0)

    @pl.when(over_up)
    def _():
        pl.semaphore_signal(barrier, inc=1, device_id=place(me, lat + 1), device_id_type=MESH)

    @pl.when(over_down)
    def _():
        pl.semaphore_signal(barrier, inc=1, device_id=place(me, lat - 1), device_id_type=MESH)

    smalls = [
        pltpu.make_async_copy(source, kept, small_sem.at[at])
        for at, (source, kept) in enumerate(
            (
                (mix_hbm, mix_ref),
                (filt_hbm, filt_ref),
                (taps_hbm, taps_ref),
                (time_hbm, time_ref),
                (area_hbm, area_ref),
            )
        )
    ]
    for small in smalls:
        small.start()
    own_copy = pltpu.make_async_copy(members_ref.at[:, 0], own, own_sem)
    own_copy.start()

    def cand_copy(s):
        r, lon = block_place(block_of(s, me))
        return pltpu.make_async_copy(
            truth_ref.at[:, r, :, pl.ds(pl.multiple_of(lon * LANE, LANE), LANE)], cand.at[s], cand_sem.at[s]
        )

    def extra_copy():
        r, _ = block_place(BLOCKS - 1)
        return pltpu.make_async_copy(
            truth_ref.at[:, r, :, pl.ds((NB - 1) * LANE, LANE)], cand.at[slots], cand_sem.at[slots]
        )

    for s in range(slots):
        cand_copy(s).start()

    @pl.when(me == extra)
    def _():
        extra_copy().start()

    greeted = n_ens - 1 + group - 1 + tall - 1
    pl.semaphore_wait(barrier, greeted + over_up.astype(jnp.int32) + over_down.astype(jnp.int32))

    def halo_copy(side, step):
        row = REACH - 1 - step if side == 0 else step
        to = lat + 1 if side == 0 else lat - 1
        return pltpu.make_async_remote_copy(
            src_ref=members_ref.at[row + 1 - side, 0],
            dst_ref=halo.at[side, row],
            send_sem=halo_send.at[side, step],
            recv_sem=halo_recv.at[side, step],
            device_id=place(me, to),
            device_id_type=MESH,
        )

    def send_side(side):
        for step in range(REACH):
            halo_copy(side, step).start()

    @pl.when((core == 1) & has_up)
    def _():
        send_side(0)

    @pl.when((core == 0) & has_down)
    def _():
        send_side(1)

    @pl.when((core == 0) & has_up)
    def _():
        send_side(0)

    @pl.when((core == 1) & has_down)
    def _():
        send_side(1)

    for small in smalls:
        small.wait()

    for k in range(K):
        mdup[k] = jnp.concatenate([mix_ref[k], mix_ref[k]], axis=1)

    def row_of(width, low, high):
        lane = lax.broadcasted_iota(jnp.int32, (1, width), 1)
        q = low + lane // C
        return jnp.where(q < high, q, -1)

    q_own = jnp.minimum(row_of(OWN_PAD, REACH, REACH + ROWS + 1), REACH + ROWS - 1)
    q_sides = (row_of(SIDE, 0, REACH), row_of(SIDE, REACH + ROWS, ROWS + 2 * REACH))

    for i in range(ROWS * TAPS * LW):
        rows_in[i : i + 1, :K] = filt_ref[i]
    turned = jnp.transpose(rows_in[...])[:KP]

    for r in range(ROWS):
        hits = [
            [(q == taps_ref[r, 0, t] - first + REACH).astype(F32) for t in range(TAPS)] for q in (q_own, *q_sides)
        ]
        for d in range(LW):
            columns = [(r * TAPS + t) * LW + d for t in range(TAPS)]
            columns = [jnp.broadcast_to(turned[:, at : at + 1], (KP, LANE)) for at in columns]
            for ref, hit in zip((a_own, a_side.at[0], a_side.at[1]), hits):
                for at in range(0, ref.shape[2], LANE):
                    terms = [columns[t] * hit[t][:, at : at + LANE] for t in range(TAPS)]
                    ref[r * LW + d, :, at : at + LANE] = functools.reduce(jnp.add, terms)

    def weights(rd, a_at, width):
        for at in range(0, width, LANE):
            total = None
            for k in range(K):
                term = a_at[rd, k : k + 1, at : at + LANE] * mdup[k]
                total = term if total is None else total + term
            yield at, split(total)

    in_low = lax.broadcasted_iota(jnp.int32, (C, LANE), 1) < C

    @pl.loop(0, ROWS * LW)
    def _(rd):
        rows = pl.ds(pl.multiple_of(rd * C, C), C)
        for at, (hi, lo) in weights(rd, a_own, OWN_PAD):
            if at < SIDE:
                w_own[rows, at : at + LANE] = hi
                w_own[rows, SIDE + at : SIDE + at + LANE] = hi
                w_own[rows, 2 * SIDE + at : 2 * SIDE + at + LANE] = lo
            else:
                w_own[rows, 3 * SIDE : 3 * SIDE + LANE] = hi
                w_own[rows, 3 * SIDE + LANE :] = jnp.where(in_low, lo, jnp.zeros_like(lo))

    own_copy.wait()
    hi, lo = split(own[:REACH].reshape(SIDE, NLON))
    own_x[:SIDE] = hi
    own_x[SIDE : 2 * SIDE] = lo
    own_x[2 * SIDE : 3 * SIDE] = hi
    hi, lo = split(own[REACH])
    own_x[3 * SIDE : 3 * SIDE + C] = hi
    own_x[3 * SIDE + C : 3 * SIDE + 2 * C] = lo
    own_x[3 * SIDE + 2 * C : 3 * SIDE + 3 * C] = hi
    own_x[3 * SIDE + 3 * C :] = jnp.zeros((C, NLON), BF16)

    @pl.loop(0, ROWS)
    def _(r):
        rows = pl.ds(pl.multiple_of(r * BAND, BAND), BAND)
        for start, width in CHUNKS:
            lons = pl.ds(start, width)
            acc[rows, lons] = dot(w_own[rows, :], own_x[:, lons])

    def side_weights(side):
        a_at = a_side.at[side]

        @pl.loop(0, REACH * LW)
        def _(i):
            rows = pl.ds(pl.multiple_of(i * C, C), C)
            for at, (hi, lo) in weights(i + side * LW, a_at, SIDE):
                w_side[rows, at : at + LANE] = hi
                w_side[rows, SIDE + at : SIDE + at + LANE] = hi
                w_side[rows, 2 * SIDE + at : 2 * SIDE + at + LANE] = lo

    def add_row(side, i, x_ref):
        rows = pl.ds(pl.multiple_of(i * BAND, BAND), BAND)
        acc_rows = pl.ds(pl.multiple_of((i + side) * BAND, BAND), BAND)
        for start, width in CHUNKS:
            lons = pl.ds(start, width)
            acc[acc_rows, lons] += dot(w_side[rows, :], x_ref[:, lons])

    side_weights(near)
    far_x[...] = jnp.zeros_like(far_x)
    for side in range(2):

        @pl.when(near == side)
        def _():
            for step in range(REACH):
                halo_copy(side, step).wait_recv()

    hi, lo = split(halo[near].reshape(SIDE, NLON))
    near_x[:SIDE] = hi
    near_x[SIDE : 2 * SIDE] = lo
    near_x[2 * SIDE :] = hi

    @pl.loop(0, REACH)
    def _(i):
        add_row(near, i, near_x)

    side_weights(far)

    def pick_target(s, r):
        time = time_ref[r]
        picked = cand[s, 0]
        for t in range(1, 4):
            picked = jnp.where(time == t, cand[s, t], picked)
        target[s] = picked

    for s in range(slots):
        cand_copy(s).wait()
        pick_target(s, block_place(block_of(s, me))[0])

    @pl.when(me == extra)
    def _():
        extra_copy().wait()
        pick_target(slots, block_place(BLOCKS - 1)[0])

    lane = lax.broadcasted_iota(jnp.int32, (C, LANE), 1)

    def fwd_copy(s, to, source):
        return pltpu.make_async_remote_copy(
            src_ref=states.at[block_of(s, to)] if s < slots else states.at[BLOCKS - 1],
            dst_ref=recv.at[s, source],
            send_sem=fwd_send.at[s, to],
            recv_sem=fwd_recv.at[s, source],
            device_id=place(to, lat),
            device_id_type=MESH,
        )

    def send_block(b):
        s, j = divmod(b, n_ens)
        to = j % 2 * half + j // 2 if s < slots else extra

        @pl.when(me != to)
        def _():
            fwd_copy(s, to, me).start()

        @pl.when(me == to)
        def _():
            recv[s, me] = states[b]

    def finish(order):
        r, _ = block_place(order * NB)

        def part(d, at):
            rows = pl.ds(pl.multiple_of(r * BAND + d * C, C), C)
            at = at % NB
            return acc[rows, at * LANE : (at + 1) * LANE]

        for lon in range(NB):
            total = part(2, lon)
            for d in (0, 1, 3, 4):
                shift = d - LW // 2
                if shift > 0:
                    mine = jnp.where(lane < shift, part(d, lon + 1), part(d, lon))
                else:
                    mine = jnp.where(lane >= LANE + shift, part(d, lon - 1), part(d, lon))
                total = total + pltpu.roll(mine, (-shift) % LANE, 1)
            cube = total + 0.044715 * total * total * total
            gelu = 0.5 * total * (1.0 + jnp.tanh(math.sqrt(2.0 / math.pi) * cube))
            states[order * NB + lon] = own[r, :, lon * LANE : (lon + 1) * LANE] + gelu
            send_block(order * NB + lon)

    finish(0)
    for step in range(REACH):
        for side, there in ((0, has_down), (1, has_up)):

            @pl.when((far == side) & there)
            def _():
                halo_copy(side, step).wait_recv()
                row = REACH - 1 - step if side == 0 else step
                hi, lo = split(halo[side, row])
                far_x[row * C : (row + 1) * C] = hi
                far_x[SIDE + row * C : SIDE + (row + 1) * C] = lo
                far_x[2 * SIDE + row * C : 2 * SIDE + (row + 1) * C] = hi

        add_row(far, jnp.where(far == 0, REACH - 1 - step, step), far_x)
        finish(step + 1)

    pairs = [(a, b) for a in range(n_ens) for b in range(a + 1, n_ens)]

    def back_copy(s, b, r, lon, to):
        return pltpu.make_async_remote_copy(
            src_ref=grads.at[s, to],
            dst_ref=out_ref.at[r, 0, :, pl.ds(pl.multiple_of(lon * LANE, LANE), LANE)],
            send_sem=back_send.at[s, to],
            recv_sem=back_recv.at[b],
            device_id=place(to, lat),
            device_id_type=MESH,
        )

    def self_copy(s, r, lon):
        return pltpu.make_async_copy(
            grads.at[s, me],
            out_ref.at[r, 0, :, pl.ds(pl.multiple_of(lon * LANE, LANE), LANE)],
            self_sem.at[s],
        )

    def measure(s, b):
        r, lon = block_place(b)
        for k in range(1, n_ens):
            fwd_copy(s, me, ens_peer(k)).wait_recv()
        area = area_ref[first + r]

        def square(v, sums):
            rows = pl.ds(pl.multiple_of(v * 8, 8), 8)
            x = [recv[s, m, rows, :] for m in range(n_ens)]
            goal = target[s, rows, :]
            gaps = [xm - goal for xm in x] + [x[a] - x[c] for a, c in pairs]
            return tuple(total + gap * gap for total, gap in zip(sums, gaps))

        zero = jnp.zeros((8, LANE), F32)
        sums = lax.fori_loop(0, C // 8, square, (zero,) * (n_ens + len(pairs)))
        skill_sum = jnp.zeros((1, LANE), F32)
        pair_sum = jnp.zeros((1, LANE), F32)
        for at, total in enumerate(sums):
            mean = jnp.sum(total, axis=0, keepdims=True) * (1.0 / C) + 1.0
            inverse = lax.rsqrt(mean)
            if at < n_ens:
                skill_sum = skill_sum + mean * inverse
                pulls[s, at] = jnp.broadcast_to(inverse * area, (8, LANE))
            else:
                pair_sum = pair_sum + mean * inverse
                pulls[s, at] = jnp.broadcast_to(inverse * (area * (1.0 / n_ens)), (8, LANE))
        cell = skill_sum * (1.0 / n_ens) - (2.0 * pair_sum + n_ens) * (1.0 / (2 * n_ens * n_ens))
        return jnp.broadcast_to(area * cell, (8, LANE))

    def give_back(s, b):
        r, lon = block_place(b)

        @pl.loop(0, C // 8)
        def _(v):
            rows = pl.ds(pl.multiple_of(v * 8, 8), 8)
            x = [recv[s, m, rows, :] for m in range(n_ens)]
            goal = target[s, rows, :]
            g = [(x[m] - goal) * pulls[s, m] for m in range(n_ens)]
            for at, (a, c) in enumerate(pairs):
                pull = (x[a] - x[c]) * pulls[s, n_ens + at]
                g[a] = g[a] - pull
                g[c] = g[c] + pull
            for m in range(n_ens):
                grads[s, m, rows, :] = g[m]

        for k in far_first(n_ens):
            back_copy(s, b, r, lon, ens_peer(k)).start()
        self_copy(s, r, lon).start()

    class Level:
        def __init__(self, buf, send, got, count, mine, peer):
            self.buf, self.send, self.got = buf, send, got
            self.count, self.mine, self.peer = count, mine, peer

        def copy(self, k, slot):
            return pltpu.make_async_remote_copy(
                src_ref=self.buf.at[self.mine],
                dst_ref=self.buf.at[slot],
                send_sem=self.send.at[k],
                recv_sem=self.got.at[slot],
                device_id=self.peer(k),
                device_id_type=MESH,
            )

        def start(self):
            for k in far_first(self.count):
                self.copy(k, self.mine).start()

        def total(self):
            for k in range(1, self.count):
                self.copy(k, lax.rem(self.mine + k, self.count)).wait_recv()
            total = self.buf[0]
            for k in range(1, self.count):
                total = total + self.buf[k]
            return total

        def sent(self):
            for k in range(1, self.count):
                self.copy(k, self.mine).wait_send()

    level1 = Level(lossbuf1, l1_send, l1_recv, n_ens, me, lambda k: place(ens_peer(k), lat))
    level2 = Level(lossbuf2, l2_send, l2_recv, group, inner, lambda k: place(me, inner_peer(k)))
    level3 = Level(lossbuf3, l3_send, l3_recv, tall, outer, lambda k: place(me, outer_peer(k)))

    part = measure(0, block_of(0, me))
    give_back(0, block_of(0, me))
    part = part + measure(1, block_of(1, me))
    part = part + measure(2, block_of(2, me))
    lossbuf2[inner] = part

    @pl.when(me == extra)
    def _():
        lossbuf2[inner] += measure(slots, BLOCKS - 1)

    level2.start()
    give_back(1, block_of(1, me))
    lossbuf3[outer] = level2.total()
    level3.start()
    give_back(2, block_of(2, me))

    @pl.when(me == extra)
    def _():
        give_back(slots, BLOCKS - 1)

    lossbuf1[me] = level3.total()
    level1.start()
    total = level1.total()
    loss_ref[0] = jnp.sum(total[0:1, :]) * (1.0 / (n_lat * ROWS * NLON))

    for s in range(slots):
        b = block_of(s, me)
        self_copy(s, *block_place(b)).wait()
        for k in range(1, n_ens):
            to = ens_peer(k)
            c = block_of(s, to)
            back_copy(s, c, *block_place(c), me).wait_recv()
            back_copy(s, b, *block_place(b), to).wait_send()
            fwd_copy(s, to, me).wait_send()
    last = BLOCKS - 1

    @pl.when(me == extra)
    def _():
        self_copy(slots, *block_place(last)).wait()
        for k in range(1, n_ens):
            back_copy(slots, last, *block_place(last), ens_peer(k)).wait_send()

    @pl.when(me != extra)
    def _():
        back_copy(slots, last, *block_place(last), me).wait_recv()
        fwd_copy(slots, extra, me).wait_send()

    for level in (level1, level2, level3):
        level.sent()

    def sent(side, there):
        @pl.when(there)
        def _():
            for step in range(REACH):
                halo_copy(side, step).wait_send()

    sent(0, has_up)
    sent(1, has_down)


def area_weights(total_rows):
    latitude = (np.arange(total_rows, dtype=np.float64) + 0.5) * (math.pi / total_rows) - 0.5 * math.pi
    cosine = np.cos(latitude)
    return (cosine / np.mean(cosine)).astype(np.float32)


def per_device(n_ens, n_lat, members, truth, target_time, row_taps, filters, mixing):
    taps = jnp.transpose(row_taps, (1, 0, 2))
    spread = jnp.transpose(filters, (1, 2, 4, 0, 3)).reshape(ROWS * TAPS * LW, 1, K)
    mix = jnp.transpose(mixing[0], (1, 0, 2))
    area = jnp.asarray(area_weights(n_lat * ROWS))
    slots = BLOCKS // n_ens
    group = min(8, n_lat)
    tall = n_lat // group
    vmem = pltpu.VMEM
    dma = pltpu.SemaphoreType.DMA
    smem = pltpu.SMEM
    smem_spec = pl.BlockSpec(memory_space=pltpu.SMEM)
    any_spec = pl.BlockSpec(memory_space=pl.ANY)
    hbm_spec = pl.BlockSpec(memory_space=pltpu.HBM)
    return pl.pallas_call(
        functools.partial(kernel, n_ens, n_lat),
        out_shape=(
            pltpu.VMEM((ROWS, 1, C, NLON), F32),
            jax.ShapeDtypeStruct((1,), F32),
        ),
        in_specs=[hbm_spec] * 7,
        out_specs=(any_spec, smem_spec),
        scratch_shapes=[
            smem((ROWS, 1, TAPS), jnp.int32),
            smem((ROWS,), jnp.int32),
            smem((n_lat * ROWS,), F32),
            vmem((ROWS * TAPS * LW, 1, K), F32),
            vmem((K, C, C), F32),
            vmem((ROWS, C, NLON), F32),
            vmem((2, REACH, C, NLON), F32),
            vmem((4 * SIDE, NLON), BF16),
            vmem((3 * SIDE, NLON), BF16),
            vmem((3 * SIDE, NLON), BF16),
            vmem((LANE, LANE), F32),
            vmem((K, C, LANE), F32),
            vmem((ROWS * LW, KP, OWN_PAD), F32),
            vmem((2, ROWS * LW, KP, SIDE), F32),
            vmem((ROWS * BAND, 4 * SIDE), BF16),
            vmem((REACH * BAND, 3 * SIDE), BF16),
            vmem((ROWS * BAND, NLON), F32),
            vmem((BLOCKS, C, LANE), F32),
            vmem((slots + 1, n_ens, C, LANE), F32),
            vmem((slots + 1, n_ens, C, LANE), F32),
            vmem((slots + 1, 4, C, LANE), F32),
            vmem((slots + 1, C, LANE), F32),
            vmem((slots + 1, n_ens * (n_ens + 1) // 2, 8, LANE), F32),
            vmem((n_ens, 8, LANE), F32),
            vmem((group, 8, LANE), F32),
            vmem((tall, 8, LANE), F32),
            dma((5,)),
            dma,
            dma((slots + 1,)),
            dma((2, REACH)),
            dma((2, REACH)),
            dma((slots + 1, n_ens)),
            dma((slots + 1, n_ens)),
            dma((slots + 1, n_ens)),
            dma((BLOCKS,)),
            dma((slots + 1,)),
            dma((n_ens,)),
            dma((n_ens,)),
            dma((group,)),
            dma((group,)),
            dma((tall,)),
            dma((tall,)),
        ],
        compiler_params=pltpu.CompilerParams(
            collective_id=0, has_side_effects=True, vmem_limit_bytes=54 * 2**20
        ),
        cost_estimate=pl.CostEstimate(flops=5_000_000_000, bytes_accessed=4_000_000, transcendentals=400_000),
    )(taps, target_time, area, spread, mix, members, truth)


def solution(mesh):
    placed = (
        P("lat", "ens", None, None),
        P(None, "lat", None, None),
        P("lat"),
        P(None, "lat", None),
        P(None, "lat", None, None, None),
        P(),
    )
    return jax.shard_map(
        functools.partial(per_device, mesh.shape["ens"], mesh.shape["lat"]),
        mesh=mesh,
        in_specs=placed,
        out_specs=(P("lat", "ens", None, None), P()),
        check_vma=False,
    )
```

```python
import functools
import math

import jax
import jax.numpy as jnp
import numpy as np
from jax import lax
from jax.experimental import pallas as pl
from jax.experimental.pallas import tpu as pltpu
from jax.sharding import PartitionSpec as P

C = 64
NLON = 640
K = 9
KP = 16
TAPS = 5
LW = 5
REACH = 4
ROWS = 5
LANE = 128
NB = NLON // LANE
BLOCKS = ROWS * NB
SIDE = REACH * C
OWN = ROWS * C
OWN_PAD = 384
BAND = LW * C
MESH = pl.DeviceIdType.MESH
CHUNKS = ((0, 256), (256, 256), (512, 128))
F32 = jnp.float32
BF16 = jnp.bfloat16


def split(x):
    hi = x.astype(BF16)
    return hi, (x - hi.astype(F32)).astype(BF16)


def dot(w, x):
    return jnp.dot(w, x, preferred_element_type=F32)


def far_first(count):
    return sorted(range(1, count), key=lambda k: -min(k, count - k))


def place_of(core, b):
    order = b // NB
    return jnp.where(core == 0, ROWS - 1 - order, order), lax.rem(b, NB)


def kernel(
    n_ens,
    n_lat,
    taps_hbm,
    time_hbm,
    area_hbm,
    filt_hbm,
    mix_hbm,
    members_ref,
    truth_ref,
    out_ref,
    loss_ref,
    taps_ref,
    time_ref,
    area_ref,
    filt_ref,
    mix_ref,
    own,
    halo,
    own_x,
    near_x,
    far_x,
    rows_in,
    mdup,
    a_own,
    a_side,
    w_own,
    w_side,
    acc,
    states,
    recv,
    grads,
    cand,
    target,
    pulls,
    lossbuf1,
    lossbuf2,
    lossbuf3,
    small_sem,
    own_sem,
    cand_sem,
    halo_send,
    halo_recv,
    fwd_send,
    fwd_recv,
    back_send,
    back_recv,
    self_sem,
    l1_send,
    l1_recv,
    l2_send,
    l2_recv,
    l3_send,
    l3_recv,
):
    me = lax.axis_index("ens")
    lat = lax.axis_index("lat")
    group = min(8, n_lat)
    tall = n_lat // group
    first = lat * ROWS
    core = lax.rem(lat, 2)
    near = 1 - core
    far = core
    slots = BLOCKS // n_ens
    extra = lax.rem(core * (n_ens // 2) + lax.rem(lat // 2, n_ens // 2), n_ens)
    inner = lax.rem(lat, group)
    outer = lat // group
    has_up = lat < n_lat - 1
    has_down = lat > 0

    half = n_ens // 2
    block_place = functools.partial(place_of, core)

    def block_of(s, owner):
        return n_ens * s + lax.rem(owner, half) * 2 + owner // half

    def place(ens_at, lat_at):
        return {"ens": ens_at, "lat": lat_at}

    def ens_peer(k):
        return lax.rem(me + k, n_ens)

    def inner_peer(k):
        return outer * group + lax.rem(inner + k, group)

    def outer_peer(k):
        return lax.rem(outer + k, tall) * group + inner

    barrier = pltpu.get_barrier_semaphore()
    for k in far_first(group):
        pl.semaphore_signal(barrier, inc=1, device_id=place(me, inner_peer(k)), device_id_type=MESH)
    for k in far_first(n_ens):
        pl.semaphore_signal(barrier, inc=1, device_id=place(ens_peer(k), lat), device_id_type=MESH)
    for k in range(1, tall):
        pl.semaphore_signal(barrier, inc=1, device_id=place(me, outer_peer(k)), device_id_type=MESH)
    over_up = has_up & (inner == group - 1)
    over_down = has_down & (inner == 0)

    @pl.when(over_up)
    def _():
        pl.semaphore_signal(barrier, inc=1, device_id=place(me, lat + 1), device_id_type=MESH)

    @pl.when(over_down)
    def _():
        pl.semaphore_signal(barrier, inc=1, device_id=place(me, lat - 1), device_id_type=MESH)

    smalls = [
        pltpu.make_async_copy(source, kept, small_sem.at[at])
        for at, (source, kept) in enumerate(
            (
                (mix_hbm, mix_ref),
                (filt_hbm, filt_ref),
                (taps_hbm, taps_ref),
                (time_hbm, time_ref),
                (area_hbm, area_ref),
            )
        )
    ]
    for small in smalls:
        small.start()
    own_copy = pltpu.make_async_copy(members_ref.at[:, 0], own, own_sem)
    own_copy.start()

    def cand_copy(s):
        r, lon = block_place(block_of(s, me))
        return pltpu.make_async_copy(
            truth_ref.at[:, r, :, pl.ds(pl.multiple_of(lon * LANE, LANE), LANE)], cand.at[s], cand_sem.at[s]
        )

    def extra_copy():
        r, _ = block_place(BLOCKS - 1)
        return pltpu.make_async_copy(
            truth_ref.at[:, r, :, pl.ds((NB - 1) * LANE, LANE)], cand.at[slots], cand_sem.at[slots]
        )

    for s in range(slots):
        cand_copy(s).start()

    @pl.when(me == extra)
    def _():
        extra_copy().start()

    greeted = n_ens - 1 + group - 1 + tall - 1
    pl.semaphore_wait(barrier, greeted + over_up.astype(jnp.int32) + over_down.astype(jnp.int32))

    def halo_copy(side, step):
        row = REACH - 1 - step if side == 0 else step
        to = lat + 1 if side == 0 else lat - 1
        return pltpu.make_async_remote_copy(
            src_ref=members_ref.at[row + 1 - side, 0],
            dst_ref=halo.at[side, row],
            send_sem=halo_send.at[side, step],
            recv_sem=halo_recv.at[side, step],
            device_id=place(me, to),
            device_id_type=MESH,
        )

    def send_side(side):
        for step in range(REACH):
            halo_copy(side, step).start()

    @pl.when((core == 1) & has_up)
    def _():
        send_side(0)

    @pl.when((core == 0) & has_down)
    def _():
        send_side(1)

    @pl.when((core == 0) & has_up)
    def _():
        send_side(0)

    @pl.when((core == 1) & has_down)
    def _():
        send_side(1)

    for small in smalls:
        small.wait()

    for k in range(K):
        mdup[k] = jnp.concatenate([mix_ref[k], mix_ref[k]], axis=1)

    def row_of(width, low, high):
        lane = lax.broadcasted_iota(jnp.int32, (1, width), 1)
        q = low + lane // C
        return jnp.where(q < high, q, -1)

    q_own = jnp.minimum(row_of(OWN_PAD, REACH, REACH + ROWS + 1), REACH + ROWS - 1)
    q_sides = (row_of(SIDE, 0, REACH), row_of(SIDE, REACH + ROWS, ROWS + 2 * REACH))

    for i in range(ROWS * TAPS * LW):
        rows_in[i : i + 1, :K] = filt_ref[i]
    turned = jnp.transpose(rows_in[...])[:KP]

    for r in range(ROWS):
        hits = [
            [(q == taps_ref[r, 0, t] - first + REACH).astype(F32) for t in range(TAPS)] for q in (q_own, *q_sides)
        ]
        for d in range(LW):
            columns = [(r * TAPS + t) * LW + d for t in range(TAPS)]
            columns = [jnp.broadcast_to(turned[:, at : at + 1], (KP, LANE)) for at in columns]
            for ref, hit in zip((a_own, a_side.at[0], a_side.at[1]), hits):
                for at in range(0, ref.shape[2], LANE):
                    terms = [columns[t] * hit[t][:, at : at + LANE] for t in range(TAPS)]
                    ref[r * LW + d, :, at : at + LANE] = functools.reduce(jnp.add, terms)

    def weights(rd, a_at, width):
        for at in range(0, width, LANE):
            total = None
            for k in range(K):
                term = a_at[rd, k : k + 1, at : at + LANE] * mdup[k]
                total = term if total is None else total + term
            yield at, split(total)

    in_low = lax.broadcasted_iota(jnp.int32, (C, LANE), 1) < C

    @pl.loop(0, ROWS * LW)
    def _(rd):
        rows = pl.ds(pl.multiple_of(rd * C, C), C)
        for at, (hi, lo) in weights(rd, a_own, OWN_PAD):
            if at < SIDE:
                w_own[rows, at : at + LANE] = hi
                w_own[rows, SIDE + at : SIDE + at + LANE] = hi
                w_own[rows, 2 * SIDE + at : 2 * SIDE + at + LANE] = lo
            else:
                w_own[rows, 3 * SIDE : 3 * SIDE + LANE] = hi
                w_own[rows, 3 * SIDE + LANE :] = jnp.where(in_low, lo, jnp.zeros_like(lo))

    own_copy.wait()
    hi, lo = split(own[:REACH].reshape(SIDE, NLON))
    own_x[:SIDE] = hi
    own_x[SIDE : 2 * SIDE] = lo
    own_x[2 * SIDE : 3 * SIDE] = hi
    hi, lo = split(own[REACH])
    own_x[3 * SIDE : 3 * SIDE + C] = hi
    own_x[3 * SIDE + C : 3 * SIDE + 2 * C] = lo
    own_x[3 * SIDE + 2 * C : 3 * SIDE + 3 * C] = hi
    own_x[3 * SIDE + 3 * C :] = jnp.zeros((C, NLON), BF16)

    @pl.loop(0, ROWS)
    def _(r):
        rows = pl.ds(pl.multiple_of(r * BAND, BAND), BAND)
        for start, width in CHUNKS:
            lons = pl.ds(start, width)
            acc[rows, lons] = dot(w_own[rows, :], own_x[:, lons])

    def side_weights(side):
        a_at = a_side.at[side]

        @pl.loop(0, REACH * LW)
        def _(i):
            rows = pl.ds(pl.multiple_of(i * C, C), C)
            for at, (hi, lo) in weights(i + side * LW, a_at, SIDE):
                w_side[rows, at : at + LANE] = hi
                w_side[rows, SIDE + at : SIDE + at + LANE] = hi
                w_side[rows, 2 * SIDE + at : 2 * SIDE + at + LANE] = lo

    def add_row(side, i, x_ref):
        rows = pl.ds(pl.multiple_of(i * BAND, BAND), BAND)
        acc_rows = pl.ds(pl.multiple_of((i + side) * BAND, BAND), BAND)
        for start, width in CHUNKS:
            lons = pl.ds(start, width)
            acc[acc_rows, lons] += dot(w_side[rows, :], x_ref[:, lons])

    side_weights(near)
    far_x[...] = jnp.zeros_like(far_x)
    for side in range(2):

        @pl.when(near == side)
        def _():
            for step in range(REACH):
                halo_copy(side, step).wait_recv()

    hi, lo = split(halo[near].reshape(SIDE, NLON))
    near_x[:SIDE] = hi
    near_x[SIDE : 2 * SIDE] = lo
    near_x[2 * SIDE :] = hi

    @pl.loop(0, REACH)
    def _(i):
        add_row(near, i, near_x)

    side_weights(far)

    def pick_target(s, r):
        time = time_ref[r]
        picked = cand[s, 0]
        for t in range(1, 4):
            picked = jnp.where(time == t, cand[s, t], picked)
        target[s] = picked

    for s in range(slots):
        cand_copy(s).wait()
        pick_target(s, block_place(block_of(s, me))[0])

    @pl.when(me == extra)
    def _():
        extra_copy().wait()
        pick_target(slots, block_place(BLOCKS - 1)[0])

    lane = lax.broadcasted_iota(jnp.int32, (C, LANE), 1)

    def fwd_copy(s, to, source):
        return pltpu.make_async_remote_copy(
            src_ref=states.at[block_of(s, to)] if s < slots else states.at[BLOCKS - 1],
            dst_ref=recv.at[s, source],
            send_sem=fwd_send.at[s, to],
            recv_sem=fwd_recv.at[s, source],
            device_id=place(to, lat),
            device_id_type=MESH,
        )

    def send_block(b):
        s, j = divmod(b, n_ens)
        to = j % 2 * half + j // 2 if s < slots else extra

        @pl.when(me != to)
        def _():
            fwd_copy(s, to, me).start()

        @pl.when(me == to)
        def _():
            recv[s, me] = states[b]

    def finish(order):
        r, _ = block_place(order * NB)

        def part(d, at):
            rows = pl.ds(pl.multiple_of(r * BAND + d * C, C), C)
            at = at % NB
            return acc[rows, at * LANE : (at + 1) * LANE]

        for lon in ((4, 0, 1, 2, 3) if order == ROWS - 1 else range(NB)):
            total = part(2, lon)
            for d in (0, 1, 3, 4):
                shift = d - LW // 2
                if shift > 0:
                    mine = jnp.where(lane < shift, part(d, lon + 1), part(d, lon))
                else:
                    mine = jnp.where(lane >= LANE + shift, part(d, lon - 1), part(d, lon))
                total = total + pltpu.roll(mine, (-shift) % LANE, 1)
            cube = total + 0.044715 * total * total * total
            gelu = 0.5 * total * (1.0 + jnp.tanh(math.sqrt(2.0 / math.pi) * cube))
            states[order * NB + lon] = own[r, :, lon * LANE : (lon + 1) * LANE] + gelu
            send_block(order * NB + lon)

    finish(0)
    for step in range(REACH):
        for side, there in ((0, has_down), (1, has_up)):

            @pl.when((far == side) & there)
            def _():
                halo_copy(side, step).wait_recv()
                row = REACH - 1 - step if side == 0 else step
                hi, lo = split(halo[side, row])
                far_x[row * C : (row + 1) * C] = hi
                far_x[SIDE + row * C : SIDE + (row + 1) * C] = lo
                far_x[2 * SIDE + row * C : 2 * SIDE + (row + 1) * C] = hi

        add_row(far, jnp.where(far == 0, REACH - 1 - step, step), far_x)
        finish(step + 1)

    pairs = [(a, b) for a in range(n_ens) for b in range(a + 1, n_ens)]

    def back_copy(s, b, r, lon, to):
        return pltpu.make_async_remote_copy(
            src_ref=grads.at[s, to],
            dst_ref=out_ref.at[r, 0, :, pl.ds(pl.multiple_of(lon * LANE, LANE), LANE)],
            send_sem=back_send.at[s, to],
            recv_sem=back_recv.at[b],
            device_id=place(to, lat),
            device_id_type=MESH,
        )

    def self_copy(s, r, lon):
        return pltpu.make_async_copy(
            grads.at[s, me],
            out_ref.at[r, 0, :, pl.ds(pl.multiple_of(lon * LANE, LANE), LANE)],
            self_sem.at[s],
        )

    def measure(s, b):
        r, lon = block_place(b)
        for k in range(1, n_ens):
            fwd_copy(s, me, ens_peer(k)).wait_recv()
        area = area_ref[first + r]

        def square(v, sums):
            rows = pl.ds(pl.multiple_of(v * 8, 8), 8)
            x = [recv[s, m, rows, :] for m in range(n_ens)]
            goal = target[s, rows, :]
            gaps = [xm - goal for xm in x] + [x[a] - x[c] for a, c in pairs]
            return tuple(total + gap * gap for total, gap in zip(sums, gaps))

        zero = jnp.zeros((8, LANE), F32)
        sums = lax.fori_loop(0, C // 8, square, (zero,) * (n_ens + len(pairs)))
        skill_sum = jnp.zeros((1, LANE), F32)
        pair_sum = jnp.zeros((1, LANE), F32)
        for at, total in enumerate(sums):
            mean = jnp.sum(total, axis=0, keepdims=True) * (1.0 / C) + 1.0
            inverse = lax.rsqrt(mean)
            if at < n_ens:
                skill_sum = skill_sum + mean * inverse
                pulls[s, at] = jnp.broadcast_to(inverse * area, (8, LANE))
            else:
                pair_sum = pair_sum + mean * inverse
                pulls[s, at] = jnp.broadcast_to(inverse * (area * (1.0 / n_ens)), (8, LANE))
        cell = skill_sum * (1.0 / n_ens) - (2.0 * pair_sum + n_ens) * (1.0 / (2 * n_ens * n_ens))
        return jnp.broadcast_to(area * cell, (8, LANE))

    def give_back(s, b):
        r, lon = block_place(b)

        @pl.loop(0, C // 8)
        def _(v):
            rows = pl.ds(pl.multiple_of(v * 8, 8), 8)
            x = [recv[s, m, rows, :] for m in range(n_ens)]
            goal = target[s, rows, :]
            g = [(x[m] - goal) * pulls[s, m] for m in range(n_ens)]
            for at, (a, c) in enumerate(pairs):
                pull = (x[a] - x[c]) * pulls[s, n_ens + at]
                g[a] = g[a] - pull
                g[c] = g[c] + pull
            for m in range(n_ens):
                grads[s, m, rows, :] = g[m]

        for k in far_first(n_ens):
            back_copy(s, b, r, lon, ens_peer(k)).start()
        self_copy(s, r, lon).start()

    class Level:
        def __init__(self, buf, send, got, count, mine, peer):
            self.buf, self.send, self.got = buf, send, got
            self.count, self.mine, self.peer = count, mine, peer

        def copy(self, k, slot):
            return pltpu.make_async_remote_copy(
                src_ref=self.buf.at[self.mine],
                dst_ref=self.buf.at[slot],
                send_sem=self.send.at[k],
                recv_sem=self.got.at[slot],
                device_id=self.peer(k),
                device_id_type=MESH,
            )

        def start(self):
            for k in far_first(self.count):
                self.copy(k, self.mine).start()

        def total(self):
            for k in range(1, self.count):
                self.copy(k, lax.rem(self.mine + k, self.count)).wait_recv()
            total = self.buf[0]
            for k in range(1, self.count):
                total = total + self.buf[k]
            return total

        def sent(self):
            for k in range(1, self.count):
                self.copy(k, self.mine).wait_send()

    level1 = Level(lossbuf1, l1_send, l1_recv, n_ens, me, lambda k: place(ens_peer(k), lat))
    level2 = Level(lossbuf2, l2_send, l2_recv, group, inner, lambda k: place(me, inner_peer(k)))
    level3 = Level(lossbuf3, l3_send, l3_recv, tall, outer, lambda k: place(me, outer_peer(k)))

    part = measure(0, block_of(0, me))
    give_back(0, block_of(0, me))
    part = part + measure(1, block_of(1, me))
    part = part + measure(2, block_of(2, me))
    lossbuf2[inner] = part

    @pl.when(me == extra)
    def _():
        lossbuf2[inner] += measure(slots, BLOCKS - 1)

    level2.start()
    give_back(1, block_of(1, me))
    lossbuf3[outer] = level2.total()
    level3.start()
    give_back(2, block_of(2, me))

    @pl.when(me == extra)
    def _():
        give_back(slots, BLOCKS - 1)

    lossbuf1[me] = level3.total()
    level1.start()
    total = level1.total()
    loss_ref[0] = jnp.sum(total[0:1, :]) * (1.0 / (n_lat * ROWS * NLON))

    for s in range(slots):
        b = block_of(s, me)
        self_copy(s, *block_place(b)).wait()
        for k in range(1, n_ens):
            to = ens_peer(k)
            c = block_of(s, to)
            back_copy(s, c, *block_place(c), me).wait_recv()
            back_copy(s, b, *block_place(b), to).wait_send()
            fwd_copy(s, to, me).wait_send()
    last = BLOCKS - 1

    @pl.when(me == extra)
    def _():
        self_copy(slots, *block_place(last)).wait()
        for k in range(1, n_ens):
            back_copy(slots, last, *block_place(last), ens_peer(k)).wait_send()

    @pl.when(me != extra)
    def _():
        back_copy(slots, last, *block_place(last), me).wait_recv()
        fwd_copy(slots, extra, me).wait_send()

    for level in (level1, level2, level3):
        level.sent()

    def sent(side, there):
        @pl.when(there)
        def _():
            for step in range(REACH):
                halo_copy(side, step).wait_send()

    sent(0, has_up)
    sent(1, has_down)


def area_weights(total_rows):
    latitude = (np.arange(total_rows, dtype=np.float64) + 0.5) * (math.pi / total_rows) - 0.5 * math.pi
    cosine = np.cos(latitude)
    return (cosine / np.mean(cosine)).astype(np.float32)


def per_device(n_ens, n_lat, members, truth, target_time, row_taps, filters, mixing):
    taps = jnp.transpose(row_taps, (1, 0, 2))
    spread = jnp.transpose(filters, (1, 2, 4, 0, 3)).reshape(ROWS * TAPS * LW, 1, K)
    mix = jnp.transpose(mixing[0], (1, 0, 2))
    area = jnp.asarray(area_weights(n_lat * ROWS))
    slots = BLOCKS // n_ens
    group = min(8, n_lat)
    tall = n_lat // group
    vmem = pltpu.VMEM
    dma = pltpu.SemaphoreType.DMA
    smem = pltpu.SMEM
    smem_spec = pl.BlockSpec(memory_space=pltpu.SMEM)
    any_spec = pl.BlockSpec(memory_space=pl.ANY)
    hbm_spec = pl.BlockSpec(memory_space=pltpu.HBM)
    return pl.pallas_call(
        functools.partial(kernel, n_ens, n_lat),
        out_shape=(
            pltpu.VMEM((ROWS, 1, C, NLON), F32),
            jax.ShapeDtypeStruct((1,), F32),
        ),
        in_specs=[hbm_spec] * 7,
        out_specs=(any_spec, smem_spec),
        scratch_shapes=[
            smem((ROWS, 1, TAPS), jnp.int32),
            smem((ROWS,), jnp.int32),
            smem((n_lat * ROWS,), F32),
            vmem((ROWS * TAPS * LW, 1, K), F32),
            vmem((K, C, C), F32),
            vmem((ROWS, C, NLON), F32),
            vmem((2, REACH, C, NLON), F32),
            vmem((4 * SIDE, NLON), BF16),
            vmem((3 * SIDE, NLON), BF16),
            vmem((3 * SIDE, NLON), BF16),
            vmem((LANE, LANE), F32),
            vmem((K, C, LANE), F32),
            vmem((ROWS * LW, KP, OWN_PAD), F32),
            vmem((2, ROWS * LW, KP, SIDE), F32),
            vmem((ROWS * BAND, 4 * SIDE), BF16),
            vmem((REACH * BAND, 3 * SIDE), BF16),
            vmem((ROWS * BAND, NLON), F32),
            vmem((BLOCKS, C, LANE), F32),
            vmem((slots + 1, n_ens, C, LANE), F32),
            vmem((slots + 1, n_ens, C, LANE), F32),
            vmem((slots + 1, 4, C, LANE), F32),
            vmem((slots + 1, C, LANE), F32),
            vmem((slots + 1, n_ens * (n_ens + 1) // 2, 8, LANE), F32),
            vmem((n_ens, 8, LANE), F32),
            vmem((group, 8, LANE), F32),
            vmem((tall, 8, LANE), F32),
            dma((5,)),
            dma,
            dma((slots + 1,)),
            dma((2, REACH)),
            dma((2, REACH)),
            dma((slots + 1, n_ens)),
            dma((slots + 1, n_ens)),
            dma((slots + 1, n_ens)),
            dma((BLOCKS,)),
            dma((slots + 1,)),
            dma((n_ens,)),
            dma((n_ens,)),
            dma((group,)),
            dma((group,)),
            dma((tall,)),
            dma((tall,)),
        ],
        compiler_params=pltpu.CompilerParams(
            collective_id=0, has_side_effects=True, vmem_limit_bytes=54 * 2**20
        ),
        cost_estimate=pl.CostEstimate(flops=5_000_000_000, bytes_accessed=4_000_000, transcendentals=400_000),
    )(taps, target_time, area, spread, mix, members, truth)


def solution(mesh):
    placed = (
        P("lat", "ens", None, None),
        P(None, "lat", None, None),
        P("lat"),
        P(None, "lat", None),
        P(None, "lat", None, None, None),
        P(),
    )
    return jax.shard_map(
        functools.partial(per_device, mesh.shape["ens"], mesh.shape["lat"]),
        mesh=mesh,
        in_specs=placed,
        out_specs=(P("lat", "ens", None, None), P()),
        check_vma=False,
    )
```
